32 devices in a mesh: ctx: 4 (over y, x), ffn: 8 (over z, core).
Axes of the slice: x: 2, y: 2, z: 4, core: 2. Of those that a mesh axis runs over, the one named last changes fastest.
Arguments:
- resid_in: bfloat16 [512, 4096], P(('ctx', 'ffn')), may hold values from -6 to 6
- queries: bfloat16 [512, 4096], P('ctx', 'ffn'), may hold values from -6 to 6
- keys_in: bfloat16 [512, 1024], P('ctx'), may hold values from -6 to 6
- value_rows_input: bfloat16 [512, 1024], P('ctx'), may hold values from -6 to 6
- w_out: bfloat16 [4096, 4096], P('ffn'), may hold values from -0.09375 to 0.09375
- norm_gain: float32 [4096], replicated, may hold values from 0.5 to 1.5
- w_gate: bfloat16 [4096, 7168], P(None, 'ffn'), may hold values from -0.09375 to 0.09375
- w_up: bfloat16 [4096, 7168], P(None, 'ffn'), may hold values from -0.09375 to 0.09375
- w_down: bfloat16 [7168, 4096], P('ffn'), may hold values from -0.0625 to 0.0625
- cotangent: bfloat16 [512, 4096], P(('ctx', 'ffn')), may hold values from -6 to 6
- positions: int32 [512], P('ctx'), may hold values from 0 to 511, as said below
- doc_ids: int32 [512], replicated, may hold values from 0 to 3, never falling along the last dimension, each value on 1 to 256 neighbouring positions
Outputs:
- mixed: bfloat16 [512, 4096], P(('ctx', 'ffn'))
- grad_resid: bfloat16 [512, 4096], P(('ctx', 'ffn'))
- grad_queries: bfloat16 [512, 4096], P('ctx', 'ffn')
- key_gradient_rows: float32 [512, 1024], P(('ctx', 'ffn'))
- value_gradient_rows: float32 [512, 1024], P(('ctx', 'ffn'))
- grad_gain: float32 [4096], replicated
- grad_w_out: float32 [4096, 4096], P('ffn', 'ctx')
- grad_w_gate: float32 [4096, 7168], P('ctx', 'ffn')
- grad_w_up: float32 [4096, 7168], P('ctx', 'ffn')
- grad_w_down: float32 [7168, 4096], P('ffn', 'ctx')
The draws below stay inside these ranges and needn't reach their ends.
Inputs may be any that keep to these rules, and one draw needn't show every extreme that they name: Each aligned block of 64 rows holds 64 consecutive positions in rising order, and every position occurs once.
All inputs are finite; a program needn't handle non-finite values.
Results may differ from the reference program's by a relative error of at most 0.033.
Values may be sent and summed in bfloat16 or wider, within the bound.
No kernel may reach another device: no remote copies, remote signals or barrier semaphores. Data moves between devices by JAX's collectives and lax.ppermute only.
A program may use at most 128 MiB of HBM per device.

```python
import math
import jax
import jax.numpy as jnp
import numpy as np
from jax import lax

D = 4096
QUERY_HEADS = 32
KEY_VALUE_HEADS = 8
HEAD_WIDTH = 128
FF = 7168
STRIPE = 64
TOKEN_COUNT = 512


def draw_queries(key, part):
    sampled_draw = jnp.clip(jax.random.normal(jax.random.fold_in(key, 3), (TOKEN_COUNT, QUERY_HEADS * HEAD_WIDTH), jnp.float32), -6.0, 6.0)
    return sampled_draw.astype(jnp.bfloat16)


def draw_keys_in(key, part):
    sampled_draw = jnp.clip(jax.random.normal(jax.random.fold_in(key, 5), (TOKEN_COUNT, KEY_VALUE_HEADS * HEAD_WIDTH), jnp.float32), -6.0, 6.0)
    return sampled_draw.astype(jnp.bfloat16)


def draw_positions(key, part):
    block_order = jax.random.permutation(jax.random.fold_in(key, 9), TOKEN_COUNT // STRIPE)
    within = jnp.arange(STRIPE)
    return (block_order[:, None] * STRIPE + within[None, :]).reshape(TOKEN_COUNT).astype(jnp.int32)


def levels(own_key, extent, shards, low, largest):
    def one(position, blocks):
        heights = jax.random.uniform(jax.random.fold_in(jax.random.fold_in(own_key, 6), position), (blocks,), jnp.float32, low / len(shards), largest / len(shards))
        return jnp.repeat(jnp.exp(heights), extent[position] // blocks).reshape((-1,) + (1,) * (len(extent) - position - 1))

    level = one(*shards[0])
    for cut in shards[1:]:
        level = level * one(*cut)
    return level


def profile(count, total, bound, lean):
    portions = [(1 << 20) // math.isqrt(standing ** lean) + 1 for standing in range(2, count + 1)]
    spare, given = total - bound - (count - 1), [1] * (count - 1)
    while spare > 0:
        candidates = [i for i in range(count - 1) if given[i] < bound]
        mass, left = sum([portions[i] for i in candidates]), spare
        for i in candidates:
            extra = min(bound - given[i], max(1, left * portions[i] // mass), spare)
            given[i] = given[i] + extra
            spare = spare - extra
    return np.array([bound] + given)


def uneven(stream_key, count, total, most, skew):
    if count == 2:
        one = jax.random.randint(stream_key, (), max(1, total - most), min(most, total - 1) + 1)
        return jnp.stack([one, total - one])
    sizes = jnp.asarray(profile(count, total, most, skew), jnp.int32)
    pairs = (count - 1) // 2
    source_of, receiver = sizes[1:1 + 2 * pairs:2], sizes[2:2 + 2 * pairs:2]
    slack = jnp.minimum(source_of - 1, most - receiver)
    moved = jax.random.randint(jax.random.fold_in(stream_key, 1), (pairs,), 0, 1 << 20) % (slack + 1)
    sizes = sizes.at[1:1 + 2 * pairs:2].set(source_of - moved).at[2:2 + 2 * pairs:2].set(receiver + moved)
    return sizes[jax.random.permutation(jax.random.fold_in(stream_key, 2), count)]


def gaussian(own_key, shape, scale, reach, split=(), kind=jnp.bfloat16):
    factor_of = levels(own_key, shape, split, -0.22, 0.18) if split else 1.0
    array = jax.random.normal(own_key, shape, jnp.float32) * scale * factor_of
    return jnp.minimum(jnp.maximum(array, -reach), reach).astype(kind)


def setup_inputs(seed: int = 0) -> dict:
    streams_of = jax.random.split(jax.random.key(seed), 13)
    resid_in = gaussian(streams_of[0], (TOKEN_COUNT, D), 1.0, 6.0, ((0, 32),))
    queries = draw_queries(jax.random.fold_in(streams_of[12], 71), 0)
    keys_in = draw_keys_in(jax.random.fold_in(streams_of[12], 71), 0)
    value_rows_input = gaussian(streams_of[3], (TOKEN_COUNT, KEY_VALUE_HEADS * HEAD_WIDTH), 1.0, 6.0, ((0, 4),))
    w_out = gaussian(streams_of[4], (QUERY_HEADS * HEAD_WIDTH, D), (QUERY_HEADS * HEAD_WIDTH) ** -0.5, 0.09375, ((0, 8),))
    norm_gain = jnp.clip(1.0 + 0.1 * jax.random.normal(streams_of[5], (D,), jnp.float32), 0.5, 1.5)
    w_gate = gaussian(streams_of[6], (D, FF), D ** -0.5, 0.09375, ((1, 8),))
    w_up = gaussian(streams_of[7], (D, FF), D ** -0.5, 0.09375, ((1, 8),))
    w_down = gaussian(streams_of[8], (FF, D), FF ** -0.5, 0.0625, ((0, 8),))
    cotangent = gaussian(streams_of[9], (TOKEN_COUNT, D), 1.0, 6.0, ((0, 32),))
    positions = draw_positions(jax.random.fold_in(streams_of[12], 71), 0)
    doc_ids = jnp.searchsorted(jnp.cumsum(uneven(streams_of[11], 4, TOKEN_COUNT, TOKEN_COUNT // 2, 0)), jnp.arange(TOKEN_COUNT), side="right").astype(jnp.int32)
    return dict(resid_in=resid_in, queries=queries, keys_in=keys_in, value_rows_input=value_rows_input, w_out=w_out, norm_gain=norm_gain, w_gate=w_gate, w_up=w_up, w_down=w_down, cotangent=cotangent, positions=positions, doc_ids=doc_ids)


masked_fill = -1e+30
norm_eps = 1e-05

def head_slices(queries, keys_in, value_rows_input, query_head_index):
    key_value_index = query_head_index // (QUERY_HEADS // KEY_VALUE_HEADS)
    return (lax.dynamic_slice_in_dim(queries, query_head_index * HEAD_WIDTH, HEAD_WIDTH, 1), lax.dynamic_slice_in_dim(keys_in, key_value_index * HEAD_WIDTH, HEAD_WIDTH, 1), lax.dynamic_slice_in_dim(value_rows_input, key_value_index * HEAD_WIDTH, HEAD_WIDTH, 1))

def masked_scores(q_head, k_head, visible):
    scores = jnp.dot(q_head, k_head.T, preferred_element_type=jnp.float32) * (1.0 / math.sqrt(HEAD_WIDTH))
    return jnp.where(visible, scores, masked_fill)

def attention_forward(queries, keys_in, value_rows_input, visible):

    def one_head(query_head_index):
        q_head, k_head, v_head = head_slices(queries, keys_in, value_rows_input, query_head_index)
        scores = masked_scores(q_head, k_head, visible)
        row_max = lax.optimization_barrier(jnp.max(scores, axis=1, keepdims=True))
        weights = jnp.where(visible, jnp.exp(scores - row_max), 0.0)
        row_total = lax.optimization_barrier(jnp.sum(weights, axis=1, keepdims=True))
        output = jnp.dot(weights.astype(jnp.bfloat16), v_head, preferred_element_type=jnp.float32) / row_total
        return (output.astype(jnp.bfloat16), (row_max + jnp.log(row_total))[:, 0])
    return lax.map(one_head, jnp.arange(QUERY_HEADS, dtype=jnp.int32))

def attention_backward(queries, keys_in, value_rows_input, grad_attended, log_totals, deltas, visible):
    scale_value = 1.0 / math.sqrt(HEAD_WIDTH)

    def one_head(query_head_index):
        q_head, k_head, v_head = head_slices(queries, keys_in, value_rows_input, query_head_index)
        g_head = lax.dynamic_slice_in_dim(grad_attended, query_head_index * HEAD_WIDTH, HEAD_WIDTH, 1)
        scores = masked_scores(q_head, k_head, visible)
        prob_weights = jnp.where(visible, jnp.exp(scores - log_totals[query_head_index][:, None]), 0.0)
        grad_probs = jnp.dot(g_head, v_head.T, preferred_element_type=jnp.float32)
        grad_scores = (prob_weights * (grad_probs - deltas[query_head_index][:, None])).astype(jnp.bfloat16)
        grad_q = jnp.dot(grad_scores, k_head, preferred_element_type=jnp.float32) * scale_value
        grad_k = jnp.dot(grad_scores.T, q_head, preferred_element_type=jnp.float32) * scale_value
        grad_v = jnp.dot(prob_weights.astype(jnp.bfloat16).T, g_head, preferred_element_type=jnp.float32)
        return (grad_q.astype(jnp.bfloat16), grad_k, grad_v)
    return lax.map(one_head, jnp.arange(QUERY_HEADS, dtype=jnp.int32))

def group_sum(pairs):
    total_sum = jnp.zeros((pairs[0][0].shape[0], pairs[0][1].shape[1]), jnp.float32)
    for left, right in pairs:
        total_sum = total_sum + jnp.dot(left, right, preferred_element_type=jnp.float32)
    return total_sum

def block_sum(left_rows, right_rows):
    return jnp.dot(left_rows.T, right_rows, preferred_element_type=jnp.float32)

def reference(resid_in, queries, keys_in, value_rows_input, w_out, norm_gain, w_gate, w_up, w_down, cotangent, positions, doc_ids):
    seg_rows = doc_ids[positions]
    visible = (positions[None, :] <= positions[:, None]) & (seg_rows[None, :] == seg_rows[:, None])
    head_out, log_totals = attention_forward(queries, keys_in, value_rows_input, visible)
    attended = jnp.transpose(head_out, (1, 0, 2)).reshape(TOKEN_COUNT, QUERY_HEADS * HEAD_WIDTH)
    hidden_bf = (resid_in.astype(jnp.float32) + group_sum([(attended, w_out)])).astype(jnp.bfloat16)
    hidden_f = lax.optimization_barrier(hidden_bf).astype(jnp.float32)
    inv_rms = lax.rsqrt(lax.optimization_barrier(jnp.mean(hidden_f * hidden_f, axis=1, keepdims=True)) + norm_eps)
    normed = (hidden_f * inv_rms * norm_gain).astype(jnp.bfloat16)
    gate_pre = jnp.dot(normed, w_gate, preferred_element_type=jnp.float32)
    up_proj = jnp.dot(normed, w_up, preferred_element_type=jnp.float32)
    gate_sig = jax.nn.sigmoid(gate_pre)
    activated = (gate_pre * gate_sig * up_proj).astype(jnp.bfloat16)
    mixed = (hidden_f + group_sum([(activated, w_down)])).astype(jnp.bfloat16)
    grad_act = jnp.dot(cotangent, w_down.T, preferred_element_type=jnp.float32)
    grad_up = (grad_act * gate_pre * gate_sig).astype(jnp.bfloat16)
    grad_gate = (grad_act * up_proj * gate_sig * (1.0 + gate_pre * (1.0 - gate_sig))).astype(jnp.bfloat16)
    grad_normed = group_sum([(grad_gate, w_gate.T), (grad_up, w_up.T)])
    gained = grad_normed * norm_gain
    inv_cube = inv_rms * inv_rms * inv_rms
    grad_resid = (cotangent.astype(jnp.float32) + inv_rms * gained - hidden_f * inv_cube * lax.optimization_barrier(jnp.mean(gained * hidden_f, axis=1, keepdims=True))).astype(jnp.bfloat16)
    grad_gain = lax.optimization_barrier(jnp.sum(grad_normed * hidden_f * inv_rms, axis=0))
    grad_attended = jnp.dot(grad_resid, w_out.T, preferred_element_type=jnp.float32).astype(jnp.bfloat16)
    deltas = lax.optimization_barrier(jnp.sum((grad_attended.astype(jnp.float32) * attended.astype(jnp.float32)).reshape(TOKEN_COUNT, QUERY_HEADS, HEAD_WIDTH), axis=2)).T
    grad_q_heads, key_head_gradient, value_head_gradient = attention_backward(queries, keys_in, value_rows_input, grad_attended, log_totals, deltas, visible)
    grad_queries = jnp.transpose(grad_q_heads, (1, 0, 2)).reshape(TOKEN_COUNT, QUERY_HEADS * HEAD_WIDTH)
    heads_per_group = QUERY_HEADS // KEY_VALUE_HEADS
    key_gradient_rows = jnp.transpose(key_head_gradient.reshape(KEY_VALUE_HEADS, heads_per_group, TOKEN_COUNT, HEAD_WIDTH).sum(axis=1), (1, 0, 2)).reshape(TOKEN_COUNT, KEY_VALUE_HEADS * HEAD_WIDTH)
    value_gradient_rows = jnp.transpose(value_head_gradient.reshape(KEY_VALUE_HEADS, heads_per_group, TOKEN_COUNT, HEAD_WIDTH).sum(axis=1), (1, 0, 2)).reshape(TOKEN_COUNT, KEY_VALUE_HEADS * HEAD_WIDTH)
    grad_w_out = block_sum(attended, grad_resid)
    grad_w_gate = block_sum(normed, grad_gate)
    grad_w_up = block_sum(normed, grad_up)
    grad_w_down = block_sum(activated, cotangent)
    return (mixed, grad_resid, grad_queries, key_gradient_rows, value_gradient_rows, grad_gain, grad_w_out, grad_w_gate, grad_w_up, grad_w_down)
```

```python
import functools
import math

import jax
import jax.numpy as jnp
from jax import lax
from jax.experimental import pallas as pl
from jax.experimental.pallas import tpu as pltpu
from jax.sharding import PartitionSpec as P

QUERY_HEADS = 32
KEY_VALUE_HEADS = 8
HEAD_WIDTH = 128
STRIPE = 64

masked_fill = -1e30
norm_eps = 1e-05
score_scale = 1.0 / math.sqrt(HEAD_WIDTH)

F32 = jnp.float32
BF16 = jnp.bfloat16
NN = (((1,), (0,)), ((), ()))
NT = (((1,), (1,)), ((), ()))
TN = (((0,), (0,)), ((), ()))
VMEM = pl.BlockSpec(memory_space=pltpu.VMEM)
SMEM = pl.BlockSpec(memory_space=pltpu.SMEM)
ANY = pl.BlockSpec(memory_space=pl.ANY)


def dot(a, b, dims=NN):
    return lax.dot_general(a, b, dims, preferred_element_type=F32)


def params(megabytes=48):
    return pltpu.CompilerParams(vmem_limit_bytes=megabytes * 1024 * 1024)


def log2(n):
    assert n & (n - 1) == 0
    return n.bit_length() - 1


def relative_rows(f, rows, n_f):
    share, half = rows // n_f, n_f // 2
    r = lax.broadcasted_iota(jnp.int32, (rows, rows), 0)
    natural = lax.broadcasted_iota(jnp.int32, (rows, rows), 1)
    j = lax.shift_right_logical(r, log2(share))
    k = lax.shift_left(j & (half - 1), 1) | lax.shift_right_logical(j, log2(half))
    return natural == lax.shift_left(k ^ f, log2(share)) + (r & (share - 1))


def visibility(same_row, pieces, doc_ref, rows):
    pos = []
    for piece in pieces:
        coded = piece[2 * rows :, :].astype(F32)
        pos.append(coded[0:1] * STRIPE + coded[1:2])
    key_pos = jnp.concatenate(pos, axis=1)
    total = doc_ref.shape[1]
    where_is = lax.broadcasted_iota(jnp.int32, (total, key_pos.shape[1]), 0).astype(F32) == key_pos
    docs = jnp.broadcast_to(doc_ref[...].astype(F32), (8, total)).astype(BF16)
    key_seg = dot(docs, where_is.astype(F32).astype(BF16))[0:1]

    def to_column(row):
        return jnp.sum(jnp.where(same_row, row[:, :rows], 0.0), axis=1, keepdims=True)

    return (key_pos <= to_column(key_pos)) & (key_seg == to_column(key_seg))


def keys_and_values(pieces, rows):
    return (
        jnp.concatenate([p[:rows] for p in pieces], axis=0),
        jnp.concatenate([p[rows : 2 * rows] for p in pieces], axis=0),
    )


def attention_kernel(n_f, n_c, f_ref, q_ref, doc_ref, w_hbm, *refs):
    pieces, (keep_ref, give_ref, att_ref, lse_ref, w_ref, sem) = refs[:n_c], refs[n_c:]
    copy = pltpu.make_async_copy(w_hbm, w_ref, sem)
    copy.start()
    rows, width = q_ref.shape
    same_row = relative_rows(f_ref[0], rows, n_f)
    visible = visibility(same_row, pieces, doc_ref, rows)
    keys, values = keys_and_values(pieces, rows)
    q = dot(same_row.astype(F32).astype(BF16), q_ref[...]).astype(BF16)
    lane = lax.broadcasted_iota(jnp.int32, (rows, HEAD_WIDTH), 1)
    log_totals = jnp.zeros((rows, HEAD_WIDTH), F32)
    for h in range(width // HEAD_WIDTH):
        cols = slice(h * HEAD_WIDTH, (h + 1) * HEAD_WIDTH)
        scores = jnp.where(visible, dot(q[:, cols], keys, NT) * score_scale, masked_fill)
        row_max = jnp.max(scores, axis=1, keepdims=True)
        weights = jnp.exp(scores - row_max)
        row_total = jnp.sum(weights, axis=1, keepdims=True)
        att_ref[:, cols] = (dot(weights.astype(BF16), values) / row_total).astype(BF16)
        log_totals = jnp.where(lane == h, row_max + jnp.log(row_total), log_totals)
    lse_ref[...] = log_totals
    copy.wait()
    att = att_ref[...]
    tile = 512
    for start in range(0, w_ref.shape[1], tile):
        out = dot(att, w_ref[:, start : start + tile]).astype(BF16)
        keep_ref[:, start : start + tile] = out[: rows // 2]
        give_ref[:, start : start + tile] = out[rows // 2 :]


def attention_call(f, queries, doc_row, w_out, pieces, n_f):
    rows, width = queries.shape
    depth = w_out.shape[1]
    half = jax.ShapeDtypeStruct((rows // 2, depth), BF16)
    return pl.pallas_call(
        functools.partial(attention_kernel, n_f, len(pieces)),
        out_shape=(
            half,
            half,
            jax.ShapeDtypeStruct((rows, width), BF16),
            jax.ShapeDtypeStruct((rows, HEAD_WIDTH), F32),
        ),
        in_specs=[SMEM, VMEM, VMEM, ANY] + [VMEM] * len(pieces),
        out_specs=[VMEM] * 4,
        scratch_shapes=[pltpu.VMEM(w_out.shape, BF16), pltpu.SemaphoreType.DMA],
        compiler_params=params(),
        name="attention_and_projection",
    )(f, queries, doc_row, w_out, *pieces)


def attention_grad_kernel(
    n_f, n_c, f_ref, q_ref, doc_ref, att_ref, lse_ref, ga_ref, gb_ref, w_hbm, *refs
):
    pieces, (dq_ref, dkv_ref, w_ref, sem) = refs[:n_c], refs[n_c:]
    copy = pltpu.make_async_copy(w_hbm, w_ref, sem)
    copy.start()
    rows, width = q_ref.shape
    same_row = relative_rows(f_ref[0], rows, n_f)
    visible = visibility(same_row, pieces, doc_ref, rows)
    keys, values = keys_and_values(pieces, rows)
    order = same_row.astype(F32).astype(BF16)
    q = dot(order, q_ref[...]).astype(BF16)
    copy.wait()
    grad_rows = jnp.concatenate([ga_ref[...], gb_ref[...]], axis=0)
    grad_att = dot(grad_rows, w_ref[...], NT).astype(BF16)
    grad_keys = jnp.zeros(keys.shape, F32)
    grad_values = jnp.zeros(keys.shape, F32)
    grad_q = []
    for h in range(width // HEAD_WIDTH):
        cols = slice(h * HEAD_WIDTH, (h + 1) * HEAD_WIDTH)
        g = grad_att[:, cols]
        scores = jnp.where(visible, dot(q[:, cols], keys, NT) * score_scale, masked_fill)
        probs = jnp.exp(scores - lse_ref[:, h : h + 1])
        delta = jnp.sum(g.astype(F32) * att_ref[:, cols].astype(F32), axis=1, keepdims=True)
        grad_scores = (probs * (dot(g, values, NT) - delta)).astype(BF16)
        grad_q.append((dot(grad_scores, keys) * score_scale).astype(BF16))
        grad_keys = grad_keys + dot(grad_scores, q[:, cols], TN)
        grad_values = grad_values + dot(probs.astype(BF16), g, TN)
    dq_ref[...] = dot(order, jnp.concatenate(grad_q, axis=1), TN).astype(BF16)
    dkv_ref[:, :HEAD_WIDTH] = (grad_keys * score_scale).astype(BF16)
    dkv_ref[:, HEAD_WIDTH:] = grad_values.astype(BF16)


def attention_grad_call(f, queries, doc_row, att, lse, grad_a, grad_b, w_out, pieces, n_f):
    rows, width = queries.shape
    return pl.pallas_call(
        functools.partial(attention_grad_kernel, n_f, len(pieces)),
        out_shape=(
            jax.ShapeDtypeStruct((rows, width), BF16),
            jax.ShapeDtypeStruct((rows * len(pieces), 2 * HEAD_WIDTH), BF16),
        ),
        in_specs=[SMEM] + [VMEM] * 6 + [ANY] + [VMEM] * len(pieces),
        out_specs=[VMEM] * 2,
        scratch_shapes=[pltpu.VMEM(w_out.shape, BF16), pltpu.SemaphoreType.DMA],
        compiler_params=params(),
        name="attention_gradients",
    )(f, queries, doc_row, att, lse, grad_a, grad_b, w_out, *pieces)


def norm_kernel(resid_ref, gain_ref, *refs):
    terms, (hidden_ref, normed_ref) = refs[:-2], refs[-2:]
    total = resid_ref[...].astype(F32)
    total = total + functools.reduce(jnp.add, [t[...].astype(F32) for t in terms])
    hidden = total.astype(BF16)
    hidden_ref[...] = hidden
    hidden = hidden.astype(F32)
    inv_rms = lax.rsqrt(jnp.mean(hidden * hidden, axis=1, keepdims=True) + norm_eps)
    normed_ref[...] = (hidden * inv_rms * gain_ref[...]).astype(BF16)


def norm_call(resid, gain_row, terms):
    out = jax.ShapeDtypeStruct(resid.shape, BF16)
    return pl.pallas_call(
        norm_kernel,
        out_shape=(out, out),
        in_specs=[VMEM] * (2 + len(terms)),
        out_specs=[VMEM] * 2,
        compiler_params=params(),
        name="residual_and_norm",
    )(resid, gain_row, *terms)


def norm_grad_kernel(cot_ref, hidden_ref, gain_ref, *refs):
    terms, (grad_ref, gain_grad_ref) = refs[:-2], refs[-2:]
    grad_normed = functools.reduce(jnp.add, [t[...].astype(F32) for t in terms])
    hidden = hidden_ref[...].astype(F32)
    inv_rms = lax.rsqrt(jnp.mean(hidden * hidden, axis=1, keepdims=True) + norm_eps)
    gained = grad_normed * gain_ref[...]
    inv_cube = inv_rms * inv_rms * inv_rms
    grad_ref[...] = (
        cot_ref[...].astype(F32)
        + inv_rms * gained
        - hidden * inv_cube * jnp.mean(gained * hidden, axis=1, keepdims=True)
    ).astype(BF16)
    gain_grad_ref[...] = jnp.sum(grad_normed * hidden * inv_rms, axis=0, keepdims=True)


def norm_grad_call(cot, hidden, gain_row, terms):
    return pl.pallas_call(
        norm_grad_kernel,
        out_shape=(
            jax.ShapeDtypeStruct(cot.shape, BF16),
            jax.ShapeDtypeStruct(gain_row.shape, F32),
        ),
        in_specs=[VMEM] * (3 + len(terms)),
        out_specs=[VMEM] * 2,
        compiler_params=params(),
        name="norm_gradients",
    )(cot, hidden, gain_row, *terms)


def gate_up_kernel(xa_ref, xb_ref, wg_ref, wu_ref, ga_ref, out_ref, gate_acc, up_acc):
    depth, width = wg_ref.shape
    half = xa_ref.shape[0]
    tile = 512
    gate_acc[...] = jnp.zeros_like(gate_acc)
    up_acc[...] = jnp.zeros_like(up_acc)

    @pl.loop(0, depth // tile)
    def _(step):
        at = pl.ds(pl.multiple_of(step * tile, tile), tile)
        x = jnp.concatenate([xa_ref[:, at], xb_ref[:, at]], axis=0)
        gate_acc[...] += dot(x, wg_ref[at, :])
        up_acc[...] += dot(x, wu_ref[at, :])

    gate, up, grad_act = gate_acc[...], up_acc[...], ga_ref[...]
    sig = jax.nn.sigmoid(gate)
    out_ref[:, :width] = (gate * sig * up).astype(BF16)
    out_ref[:, width : 2 * width] = (grad_act * up * sig * (1.0 + gate * (1.0 - sig))).astype(BF16)
    out_ref[:, 2 * width :] = (grad_act * gate * sig).astype(BF16)


def gate_up_call(xa, xb, w_gate, w_up, grad_act):
    depth, width = w_gate.shape
    rows = grad_act.shape[0]
    return pl.pallas_call(
        gate_up_kernel,
        out_shape=jax.ShapeDtypeStruct((rows, 3 * width), BF16),
        in_specs=[VMEM] * 5,
        out_specs=VMEM,
        scratch_shapes=[pltpu.VMEM((rows, width), F32)] * 2,
        compiler_params=params(24),
        name="gate_up_and_gradients",
    )(xa, xb, w_gate, w_up, grad_act)


def normed_grad_kernel(pay_ref, wg_ref, wu_ref, keep_ref, give_ref):
    depth, width = wg_ref.shape
    half = keep_ref.shape[0]
    tile = 512

    @pl.loop(0, depth // tile)
    def _(step):
        at = pl.ds(pl.multiple_of(step * tile, tile), tile)
        out = dot(pay_ref[:, width : 2 * width], wg_ref[at, :], NT)
        out = (out + dot(pay_ref[:, 2 * width :], wu_ref[at, :], NT)).astype(BF16)
        keep_ref[:, at] = out[:half]
        give_ref[:, at] = out[half:]


def normed_grad_call(pay, w_gate, w_up):
    depth, width = w_gate.shape
    rows = pay.shape[0]
    out = jax.ShapeDtypeStruct((rows // 2, depth), BF16)
    return pl.pallas_call(
        normed_grad_kernel,
        out_shape=(out, out),
        in_specs=[VMEM] * 3,
        out_specs=[VMEM] * 2,
        compiler_params=params(24),
        name="normed_gradients",
    )(pay, w_gate, w_up)


def down_kernel(pay_ref, w_ref, keep_ref, give_ref):
    out = dot(pay_ref[:, : w_ref.shape[0]], w_ref[...]).astype(BF16)
    half = keep_ref.shape[0]
    keep_ref[...] = out[:half]
    give_ref[...] = out[half:]


def down_call(pay, w_down, tile=512):
    width, depth = w_down.shape
    rows = pay.shape[0]
    o_spec = pl.BlockSpec((rows // 2, tile), lambda i: (0, i))
    out = jax.ShapeDtypeStruct((rows // 2, depth), BF16)
    return pl.pallas_call(
        down_kernel,
        grid=(depth // tile,),
        out_shape=(out, out),
        in_specs=[
            pl.BlockSpec(pay.shape, lambda i: (0, 0)),
            pl.BlockSpec((width, tile), lambda i: (0, i)),
        ],
        out_specs=[o_spec, o_spec],
        compiler_params=params(),
        name="down_projection",
    )(pay, w_down)


def body(
    resid_in,
    queries,
    keys_in,
    value_rows_input,
    w_out,
    norm_gain,
    w_gate,
    w_up,
    w_down,
    cotangent,
    positions,
    doc_ids,
):
    rows = queries.shape[0]
    heads = queries.shape[1] // HEAD_WIDTH
    n_c, n_f = lax.axis_size("ctx"), lax.axis_size("ffn")
    c, f = lax.axis_index("ctx"), lax.axis_index("ffn")
    share, half = rows // n_f, n_f // 2
    depth = resid_in.shape[1]
    hidden_units = w_gate.shape[1]
    group = f * heads // (QUERY_HEADS // KEY_VALUE_HEADS)
    f_ref = f.astype(jnp.int32).reshape(1)
    gain_row = norm_gain.reshape(1, depth)
    doc_row = doc_ids.reshape(1, -1)

    def exchange(x, axis, k):
        return lax.ppermute(x, axis, [(i, i ^ k) for i in range(lax.axis_size(axis))])

    def gather_rows(x):
        mine = jnp.concatenate([x] + [exchange(x, "ffn", 2 * m) for m in range(1, half)], axis=0)
        return mine, exchange(mine, "ffn", 1)

    def scatter_rows(keep, give):
        total = (keep.astype(F32) + exchange(give, "ffn", 1).astype(F32)).astype(BF16)
        blocks = [total[m * share : (m + 1) * share] for m in range(half)]
        return [blocks[0]] + [exchange(blocks[m], "ffn", 2 * m) for m in range(1, half)]

    def gather_ctx(x):
        return jnp.concatenate([x] + [exchange(x, "ctx", k) for k in range(1, n_c)], axis=0)

    def sum_everywhere(x):
        x = x + exchange(x, "ffn", 1)
        x = functools.reduce(jnp.add, [x] + [exchange(x, "ffn", 2 * m) for m in range(1, half)])
        return functools.reduce(jnp.add, [x] + [exchange(x, "ctx", k) for k in range(1, n_c)])

    col_count = depth // n_c

    def gather_columns(a, b):
        def part(k):
            start = (c ^ k) * col_count
            return jnp.concatenate(
                [lax.dynamic_slice_in_dim(t, start, col_count, 1) for t in (a, b)], axis=0
            )

        return jnp.concatenate([part(0)] + [exchange(part(k), "ctx", k) for k in range(1, n_c)], 0)

    def head_slice(x):
        return lax.dynamic_slice_in_dim(x, group * HEAD_WIDTH, HEAD_WIDTH, 1)

    coded = jnp.concatenate([positions // STRIPE, positions % STRIPE]).astype(BF16)
    coded = coded.reshape(2, -1)
    coded = jnp.concatenate([coded, jnp.zeros((14, coded.shape[1]), BF16)], axis=0)
    payload = jnp.concatenate([head_slice(keys_in), head_slice(value_rows_input), coded], axis=0)
    pieces = [payload] + [exchange(payload, "ctx", k) for k in range(1, n_c)]
    cot_a, cot_b = gather_rows(cotangent)

    keep, give, att, lse = attention_call(f_ref, queries, doc_row, w_out, pieces, n_f)
    hidden, normed = norm_call(resid_in, gain_row, scatter_rows(keep, give))
    normed_a, normed_b = gather_rows(normed)

    grad_act = dot(jnp.concatenate([cot_a, cot_b], axis=0), w_down, NT)
    cot_cols = gather_columns(cot_a, cot_b)
    att_all = gather_ctx(att)

    pay = gate_up_call(normed_a, normed_b, w_gate, w_up, grad_act)
    keep, give = normed_grad_call(pay, w_gate, w_up)
    terms = scatter_rows(keep, give)
    pay_all = gather_ctx(pay)
    normed_cols = gather_columns(normed_a, normed_b)
    down_keep, down_give = down_call(pay, w_down)
    grad_resid, gain_part = norm_grad_call(cotangent, hidden, gain_row, terms)
    grad_a, grad_b = gather_rows(grad_resid)
    grad_gain = sum_everywhere(gain_part).reshape(depth)

    grad_w_down = dot(pay_all[:, :hidden_units], cot_cols, TN)
    grad_w_gate = dot(normed_cols, pay_all[:, hidden_units : 2 * hidden_units], TN)
    grad_w_up = dot(normed_cols, pay_all[:, 2 * hidden_units :], TN)

    grad_queries, dkv = attention_grad_call(
        f_ref, queries, doc_row, att, lse, grad_a, grad_b, w_out, pieces, n_f
    )
    grad_cols = gather_columns(grad_a, grad_b)
    grad_w_out = dot(att_all, grad_cols, TN)

    mixed_terms = scatter_rows(down_keep, down_give)
    mixed = functools.reduce(jnp.add, [t.astype(F32) for t in mixed_terms])
    mixed = (hidden.astype(F32) + mixed).astype(BF16)

    dkv_own = dkv[:rows].astype(F32)
    for k in range(1, n_c):
        dkv_own = dkv_own + exchange(dkv[k * rows : (k + 1) * rows], "ctx", k).astype(F32)
    dkv_own = dkv_own.astype(BF16).reshape(n_f, share, 2 * HEAD_WIDTH)
    dkv_heads = lax.all_to_all(dkv_own, "ffn", 0, 0).astype(F32)
    dkv_heads = dkv_heads.reshape(
        KEY_VALUE_HEADS, n_f // KEY_VALUE_HEADS, share, 2, HEAD_WIDTH
    ).sum(axis=1)
    dkv_heads = jnp.transpose(dkv_heads, (2, 1, 0, 3)).reshape(2, share, -1)
    return (
        mixed,
        grad_resid,
        grad_queries,
        dkv_heads[0],
        dkv_heads[1],
        grad_gain,
        grad_w_out,
        grad_w_gate,
        grad_w_up,
        grad_w_down,
    )


def solution(mesh):
    return jax.shard_map(
        body,
        mesh=mesh,
        in_specs=(
            P(("ctx", "ffn"), None),
            P("ctx", "ffn"),
            P("ctx", None),
            P("ctx", None),
            P("ffn", None),
            P(),
            P(None, "ffn"),
            P(None, "ffn"),
            P("ffn", None),
            P(("ctx", "ffn"), None),
            P("ctx"),
            P(),
        ),
        out_specs=(
            P(("ctx", "ffn"), None),
            P(("ctx", "ffn"), None),
            P("ctx", "ffn"),
            P(("ctx", "ffn"), None),
            P(("ctx", "ffn"), None),
            P(),
            P("ffn", "ctx"),
            P("ctx", "ffn"),
            P("ctx", "ffn"),
            P("ffn", "ctx"),
        ),
        check_vma=False,
    )
```

```python
import functools
import math

import jax
import jax.numpy as jnp
from jax import lax
from jax.experimental import pallas as pl
from jax.experimental.pallas import tpu as pltpu
from jax.sharding import PartitionSpec as P

QUERY_HEADS = 32
KEY_VALUE_HEADS = 8
HEAD_WIDTH = 128
STRIPE = 64

masked_fill = -1e30
norm_eps = 1e-05
score_scale = 1.0 / math.sqrt(HEAD_WIDTH)

F32 = jnp.float32
BF16 = jnp.bfloat16
NN = (((1,), (0,)), ((), ()))
NT = (((1,), (1,)), ((), ()))
TN = (((0,), (0,)), ((), ()))
VMEM = pl.BlockSpec(memory_space=pltpu.VMEM)
SMEM = pl.BlockSpec(memory_space=pltpu.SMEM)
ANY = pl.BlockSpec(memory_space=pl.ANY)


def dot(a, b, dims=NN):
    return lax.dot_general(a, b, dims, preferred_element_type=F32)


def params(megabytes=48):
    return pltpu.CompilerParams(vmem_limit_bytes=megabytes * 1024 * 1024)


def cost(microseconds):
    return pl.CostEstimate(
        flops=int(microseconds * 5e8), bytes_accessed=int(microseconds * 2e6), transcendentals=0
    )


def fetch(sources, targets, sems):
    copies = [pltpu.make_async_copy(s, t, sems.at[i]) for i, (s, t) in enumerate(zip(sources, targets))]
    for copy in copies:
        copy.start()
    return copies


def scratch_like(*arrays):
    return [pltpu.VMEM(a.shape, a.dtype) for a in arrays] + [
        pltpu.SemaphoreType.DMA((len(arrays),))
    ]


def log2(n):
    assert n & (n - 1) == 0
    return n.bit_length() - 1


def relative_rows(f, rows, n_f):
    share, half = rows // n_f, n_f // 2
    r = lax.broadcasted_iota(jnp.int32, (rows, rows), 0)
    natural = lax.broadcasted_iota(jnp.int32, (rows, rows), 1)
    j = lax.shift_right_logical(r, log2(share))
    k = lax.shift_left(j & (half - 1), 1) | lax.shift_right_logical(j, log2(half))
    return natural == lax.shift_left(k ^ f, log2(share)) + (r & (share - 1))


def visibility(same_row, pieces, rows):
    coded = [piece[2 * rows :, :].astype(F32) for piece in pieces]
    key_pos = jnp.concatenate([t[0:1] * STRIPE + t[1:2] for t in coded], axis=1)
    key_seg = jnp.concatenate([t[2:3] for t in coded], axis=1)

    def to_column(row):
        return jnp.sum(jnp.where(same_row, row[:, :rows], 0.0), axis=1, keepdims=True)

    return (key_pos <= to_column(key_pos)) & (key_seg == to_column(key_seg))


def keys_and_values(pieces, rows):
    return (
        jnp.concatenate([p[:rows] for p in pieces], axis=0),
        jnp.concatenate([p[rows : 2 * rows] for p in pieces], axis=0),
    )


def prepare_kernel(
    n_f, f_ref, group_ref, q_hbm, k_hbm, v_hbm, pos_hbm, doc_hbm, q_out, payload, *scratch
):
    q_ref, pos_ref, doc_ref, sems = scratch
    rows = q_ref.shape[0]
    cols = pl.ds(pl.multiple_of(group_ref[0] * HEAD_WIDTH, HEAD_WIDTH), HEAD_WIDTH)
    copies = fetch(
        [pos_hbm, doc_hbm, q_hbm, k_hbm.at[:, cols], v_hbm.at[:, cols]],
        [pos_ref, doc_ref, q_ref, payload.at[pl.ds(0, rows)], payload.at[pl.ds(rows, rows)]],
        sems,
    )
    same_row = relative_rows(f_ref[0], rows, n_f)
    line = lax.broadcasted_iota(jnp.int32, (16, rows), 0)
    copies[0].wait()
    copies[1].wait()
    pos = pos_ref[...]
    total = doc_ref.shape[1]
    where_is = lax.broadcasted_iota(jnp.int32, (total, rows), 0) == pos
    docs = jnp.broadcast_to(doc_ref[...].astype(F32), (8, total)).astype(BF16)
    seg = dot(docs, where_is.astype(F32).astype(BF16))[0:1]
    high = lax.shift_right_logical(pos, log2(STRIPE))
    low = pos & (STRIPE - 1)
    coded = jnp.where(line == 0, high.astype(F32), jnp.where(line == 1, low.astype(F32), 0.0))
    payload[2 * rows :, :] = jnp.where(line == 2, seg, coded).astype(BF16)
    copies[2].wait()
    q_out[...] = dot(same_row.astype(F32).astype(BF16), q_ref[...]).astype(BF16)
    copies[3].wait()
    copies[4].wait()


def prepare_call(f, group, queries, keys_in, values_in, pos_row, doc_row, n_f):
    rows = queries.shape[0]
    assert rows == HEAD_WIDTH
    return pl.pallas_call(
        functools.partial(prepare_kernel, n_f),
        out_shape=(
            jax.ShapeDtypeStruct(queries.shape, BF16),
            jax.ShapeDtypeStruct((2 * rows + 16, HEAD_WIDTH), BF16),
        ),
        in_specs=[SMEM, SMEM] + [ANY] * 5,
        out_specs=[VMEM] * 2,
        scratch_shapes=scratch_like(queries, pos_row, doc_row)[:-1]
        + [pltpu.SemaphoreType.DMA((5,))],
        compiler_params=params(58),
        cost_estimate=cost(2),
        name="prepare_attention",
    )(f, group, queries, keys_in, values_in, pos_row, doc_row)


def attention_kernel(n_f, n_c, f_ref, *refs):
    sources, refs = refs[: n_c + 2], refs[n_c + 2 :]
    (keep_ref, give_ref, att_ref, lse_ref), scratch, sems = refs[:4], refs[4:-1], refs[-1]
    copies = fetch(sources, scratch, sems)
    q_ref, pieces, w_ref = scratch[0], scratch[1:-1], scratch[-1]
    for copy in copies[:-1]:
        copy.wait()
    rows, width = q_ref.shape
    same_row = relative_rows(f_ref[0], rows, n_f)
    visible = visibility(same_row, pieces, rows)
    keys, values = keys_and_values(pieces, rows)
    q = q_ref[...]
    lane = lax.broadcasted_iota(jnp.int32, (rows, HEAD_WIDTH), 1)
    log_totals = jnp.zeros((rows, HEAD_WIDTH), F32)
    for h in range(width // HEAD_WIDTH):
        cols = slice(h * HEAD_WIDTH, (h + 1) * HEAD_WIDTH)
        scores = jnp.where(visible, dot(q[:, cols], keys, NT) * score_scale, masked_fill)
        row_max = jnp.max(scores, axis=1, keepdims=True)
        weights = jnp.exp(scores - row_max)
        row_total = jnp.sum(weights, axis=1, keepdims=True)
        att_ref[:, cols] = (dot(weights.astype(BF16), values) / row_total).astype(BF16)
        log_totals = jnp.where(lane == h, row_max + jnp.log(row_total), log_totals)
    lse_ref[...] = log_totals
    copies[-1].wait()
    att = att_ref[...]
    tile = 512
    for start in range(0, w_ref.shape[1], tile):
        out = dot(att, w_ref[:, start : start + tile]).astype(BF16)
        keep_ref[:, start : start + tile] = out[: rows // 2]
        give_ref[:, start : start + tile] = out[rows // 2 :]


def attention_call(f, queries, w_out, pieces, n_f):
    rows, width = queries.shape
    depth = w_out.shape[1]
    half = jax.ShapeDtypeStruct((rows // 2, depth), BF16)
    att = jax.ShapeDtypeStruct((rows, width), BF16)
    lse = jax.ShapeDtypeStruct((rows, HEAD_WIDTH), F32)
    return pl.pallas_call(
        functools.partial(attention_kernel, n_f, len(pieces)),
        out_shape=(half, half, att, lse),
        in_specs=[SMEM] + [ANY] * (2 + len(pieces)),
        out_specs=[VMEM] * 4,
        scratch_shapes=scratch_like(queries, *pieces, w_out),
        compiler_params=params(56),
        cost_estimate=cost(4),
        name="attention_and_projection",
    )(f, queries, *pieces, w_out)


def fold(row):
    width = 2 * HEAD_WIDTH
    return [row[:, i : i + width] for i in range(0, row.shape[1], width)]


def attention_grad_kernel(n_f, n_c, f_ref, *refs):
    pieces, refs = refs[:n_c], refs[n_c:]
    q_ref, att_ref, lse_ref, gain_ref, ga_ref, gb_ref, w_ref = refs[:7]
    dq_ref, dkv_refs = refs[7], refs[8:]
    rows, width = q_ref.shape
    same_row = relative_rows(f_ref[0], rows, n_f)
    visible = visibility(same_row, pieces, rows)
    keys, values = keys_and_values(pieces, rows)
    order = same_row.astype(F32).astype(BF16)
    q = q_ref[...]
    grad_rows = jnp.concatenate([ga_ref[...], gb_ref[...]], axis=0)
    grad_att = dot(grad_rows, w_ref[...], NT).astype(BF16)
    grad_keys = jnp.zeros(keys.shape, F32)
    grad_values = jnp.zeros(keys.shape, F32)
    grad_q = []
    for h in range(width // HEAD_WIDTH):
        cols = slice(h * HEAD_WIDTH, (h + 1) * HEAD_WIDTH)
        g = grad_att[:, cols]
        scores = jnp.where(visible, dot(q[:, cols], keys, NT) * score_scale, masked_fill)
        probs = jnp.exp(scores - lse_ref[:, h : h + 1])
        delta = jnp.sum(g.astype(F32) * att_ref[:, cols].astype(F32), axis=1, keepdims=True)
        grad_scores = (probs * (dot(g, values, NT) - delta)).astype(BF16)
        grad_q.append((dot(grad_scores, keys) * score_scale).astype(BF16))
        grad_keys = grad_keys + dot(grad_scores, q[:, cols], TN)
        grad_values = grad_values + dot(probs.astype(BF16), g, TN)
    dq_ref[...] = dot(order, jnp.concatenate(grad_q, axis=1), TN).astype(BF16)
    high = gain_ref[...].astype(BF16)
    low = (gain_ref[...] - high.astype(F32)).astype(BF16)
    lines = fold(high) + fold(low)
    for k, dkv_ref in enumerate(dkv_refs):
        part = slice(k * rows, (k + 1) * rows)
        dkv_ref[:rows, :HEAD_WIDTH] = (grad_keys[part] * score_scale).astype(BF16)
        dkv_ref[:rows, HEAD_WIDTH:] = grad_values[part].astype(BF16)
        for i, line in enumerate(lines):
            dkv_ref[rows + i : rows + i + 1, :] = line


def attention_grad_call(f, queries, att, lse, gain, grad_a, grad_b, w_out, pieces, n_f):
    rows, width = queries.shape
    n_c = len(pieces)
    dkv = jax.ShapeDtypeStruct((rows + gain.shape[1] // HEAD_WIDTH, 2 * HEAD_WIDTH), BF16)
    return pl.pallas_call(
        functools.partial(attention_grad_kernel, n_f, n_c),
        out_shape=(jax.ShapeDtypeStruct((rows, width), BF16),) + (dkv,) * n_c,
        in_specs=[SMEM] + [VMEM] * (7 + n_c),
        out_specs=(VMEM,) * (1 + n_c),
        compiler_params=params(24),
        cost_estimate=cost(4),
        name="attention_gradients",
    )(f, *pieces, queries, att, lse, gain, grad_a, grad_b, w_out)


def norm_kernel(resid_ref, gain_ref, *refs):
    terms, (hidden_ref, normed_ref) = refs[:-2], refs[-2:]
    total = resid_ref[...].astype(F32)
    total = total + functools.reduce(jnp.add, [t[...].astype(F32) for t in terms])
    hidden = total.astype(BF16)
    hidden_ref[...] = hidden
    hidden = hidden.astype(F32)
    inv_rms = lax.rsqrt(jnp.mean(hidden * hidden, axis=1, keepdims=True) + norm_eps)
    normed_ref[...] = (hidden * inv_rms * gain_ref[...]).astype(BF16)


def norm_call(resid, gain_row, terms):
    out = jax.ShapeDtypeStruct(resid.shape, BF16)
    return pl.pallas_call(
        norm_kernel,
        out_shape=(out, out),
        in_specs=[VMEM] * (2 + len(terms)),
        out_specs=[VMEM] * 2,
        compiler_params=params(8),
        cost_estimate=cost(8),
        name="residual_and_norm",
    )(resid, gain_row, *terms)


def norm_grad_kernel(cot_ref, hidden_ref, gain_ref, *refs):
    terms, (grad_ref, gain_grad_ref) = refs[:-2], refs[-2:]
    grad_normed = functools.reduce(jnp.add, [t[...].astype(F32) for t in terms])
    hidden = hidden_ref[...].astype(F32)
    inv_rms = lax.rsqrt(jnp.mean(hidden * hidden, axis=1, keepdims=True) + norm_eps)
    gained = grad_normed * gain_ref[...]
    inv_cube = inv_rms * inv_rms * inv_rms
    grad_ref[...] = (
        cot_ref[...].astype(F32)
        + inv_rms * gained
        - hidden * inv_cube * jnp.mean(gained * hidden, axis=1, keepdims=True)
    ).astype(BF16)
    gain_grad_ref[...] = jnp.sum(grad_normed * hidden * inv_rms, axis=0, keepdims=True)


def norm_grad_call(cot, hidden, gain_row, terms):
    return pl.pallas_call(
        norm_grad_kernel,
        out_shape=(
            jax.ShapeDtypeStruct(cot.shape, BF16),
            jax.ShapeDtypeStruct(gain_row.shape, F32),
        ),
        in_specs=[VMEM] * (3 + len(terms)),
        out_specs=[VMEM] * 2,
        compiler_params=params(8),
        cost_estimate=cost(8),
        name="norm_gradients",
    )(cot, hidden, gain_row, *terms)


def gate_up_kernel(xa_ref, xb_ref, wg_ref, wu_ref, ga_ref, out_ref, gate_acc, up_acc):
    depth, width = wg_ref.shape
    half = xa_ref.shape[0]
    tile = 512
    gate_acc[...] = jnp.zeros_like(gate_acc)
    up_acc[...] = jnp.zeros_like(up_acc)

    @pl.loop(0, depth // tile)
    def _(step):
        at = pl.ds(pl.multiple_of(step * tile, tile), tile)
        x = jnp.concatenate([xa_ref[:, at], xb_ref[:, at]], axis=0)
        gate_acc[...] += dot(x, wg_ref[at, :])
        up_acc[...] += dot(x, wu_ref[at, :])

    gate, up, grad_act = gate_acc[...], up_acc[...], ga_ref[...]
    sig = jax.nn.sigmoid(gate)
    out_ref[:, :width] = (gate * sig * up).astype(BF16)
    out_ref[:, width : 2 * width] = (grad_act * up * sig * (1.0 + gate * (1.0 - sig))).astype(BF16)
    out_ref[:, 2 * width :] = (grad_act * gate * sig).astype(BF16)


def gate_up_call(xa, xb, w_gate, w_up, grad_act):
    depth, width = w_gate.shape
    rows = grad_act.shape[0]
    return pl.pallas_call(
        gate_up_kernel,
        out_shape=jax.ShapeDtypeStruct((rows, 3 * width), BF16),
        in_specs=[VMEM] * 5,
        out_specs=VMEM,
        scratch_shapes=[pltpu.VMEM((rows, width), F32)] * 2,
        compiler_params=params(24),
        cost_estimate=cost(2),
        name="gate_up_and_gradients",
    )(xa, xb, w_gate, w_up, grad_act)


def normed_grad_kernel(pay_ref, wg_ref, wu_ref, keep_ref, give_ref):
    depth, width = wg_ref.shape
    half = keep_ref.shape[0]
    tile = 512

    @pl.loop(0, depth // tile)
    def _(step):
        at = pl.ds(pl.multiple_of(step * tile, tile), tile)
        out = dot(pay_ref[:, width : 2 * width], wg_ref[at, :], NT)
        out = (out + dot(pay_ref[:, 2 * width :], wu_ref[at, :], NT)).astype(BF16)
        keep_ref[:, at] = out[:half]
        give_ref[:, at] = out[half:]


def normed_grad_call(pay, w_gate, w_up):
    depth, width = w_gate.shape
    rows = pay.shape[0]
    out = jax.ShapeDtypeStruct((rows // 2, depth), BF16)
    return pl.pallas_call(
        normed_grad_kernel,
        out_shape=(out, out),
        in_specs=[VMEM] * 3,
        out_specs=[VMEM] * 2,
        compiler_params=params(24),
        cost_estimate=cost(2),
        name="normed_gradients",
    )(pay, w_gate, w_up)


def column_blocks_kernel(c_ref, a_ref, *out_refs):
    cols = a_ref.shape[1] // len(out_refs)
    for k, out_ref in enumerate(out_refs):
        start = pl.multiple_of((c_ref[0] ^ k) * cols, 128)
        out_ref[...] = a_ref[:, pl.ds(start, cols)]


def column_blocks(c, a, n_c):
    rows, depth = a.shape
    return pl.pallas_call(
        column_blocks_kernel,
        out_shape=(jax.ShapeDtypeStruct((rows, depth // n_c), BF16),) * n_c,
        in_specs=[SMEM, VMEM],
        out_specs=(VMEM,) * n_c,
        compiler_params=params(8),
        cost_estimate=cost(1),
        name="column_blocks",
    )(c, a)


def take(refs, pieces, width):
    return jnp.concatenate([refs[i][r : r + n, at : at + width] for i, r, n, at in pieces], axis=0)


def weight_grad_kernel(left, right, n_left, widths, *refs):
    out_ref = refs[-1]
    rhs = take(refs[n_left:-1], right, widths[1])
    tile = 256
    for at in range(0, widths[0], tile):
        size = min(tile, widths[0] - at)
        lhs = take(refs[:n_left], [(i, r, n, first + at) for i, r, n, first in left], size)
        out_ref[at : at + size, :] = dot(lhs, rhs, TN)


def weight_grad_call(left, left_refs, right, right_refs, widths, name):
    return pl.pallas_call(
        functools.partial(weight_grad_kernel, left, right, len(left_refs), widths),
        out_shape=jax.ShapeDtypeStruct(widths, F32),
        in_specs=[VMEM] * (len(left_refs) + len(right_refs)),
        out_specs=VMEM,
        compiler_params=params(16),
        cost_estimate=cost(4),
        name=name,
    )(*left_refs, *right_refs)


def sum_kernel(n_f, rows, *refs):
    parts, out_ref = refs[:-1], refs[-1]
    share = rows // n_f
    lines = (parts[0].shape[0] - rows) // 2

    def tree(values):
        while len(values) > 1:
            values = [values[i] + values[i + 1] for i in range(0, len(values), 2)]
        return values[0]

    total = tree([p[:rows, :].astype(F32) for p in parts]).astype(BF16)
    gain = tree(
        [p[rows : rows + lines, :].astype(F32) + p[rows + lines :, :].astype(F32) for p in parts]
    )
    high = gain.astype(BF16)
    low = (gain - high.astype(F32)).astype(BF16)
    for f in range(n_f):
        out_ref[f, :lines, :] = high
        out_ref[f, lines : 2 * lines, :] = low
        out_ref[f, 2 * lines :, :] = total[f * share : (f + 1) * share]


def sum_call(parts, rows, n_f):
    lines = parts[0].shape[0] - rows
    return pl.pallas_call(
        functools.partial(sum_kernel, n_f, rows),
        out_shape=jax.ShapeDtypeStruct((n_f, lines + rows // n_f, 2 * HEAD_WIDTH), BF16),
        in_specs=[VMEM] * len(parts),
        out_specs=VMEM,
        compiler_params=params(8),
        cost_estimate=cost(1),
        name="sum_over_ctx",
    )(*parts)


def heads_kernel(n_f, in_ref, dk_ref, dv_ref, gain_ref):
    per_head = n_f // KEY_VALUE_HEADS
    width = 2 * HEAD_WIDTH
    lines = gain_ref.shape[1] // width
    for g in range(KEY_VALUE_HEADS):
        total = in_ref[g * per_head, 2 * lines :, :].astype(F32)
        for other in range(1, per_head):
            total = total + in_ref[g * per_head + other, 2 * lines :, :].astype(F32)
        dk_ref[:, g * HEAD_WIDTH : (g + 1) * HEAD_WIDTH] = total[:, :HEAD_WIDTH]
        dv_ref[:, g * HEAD_WIDTH : (g + 1) * HEAD_WIDTH] = total[:, HEAD_WIDTH:]
    gain = functools.reduce(
        jnp.add,
        [
            in_ref[f, :lines, :].astype(F32) + in_ref[f, lines : 2 * lines, :].astype(F32)
            for f in range(n_f)
        ],
    )
    for i in range(lines):
        gain_ref[:, i * width : (i + 1) * width] = gain[i : i + 1]


def heads_call(parts, depth, n_f):
    share = parts.shape[1] - depth // HEAD_WIDTH
    out = jax.ShapeDtypeStruct((share, KEY_VALUE_HEADS * HEAD_WIDTH), F32)
    return pl.pallas_call(
        functools.partial(heads_kernel, n_f),
        out_shape=(out, out, jax.ShapeDtypeStruct((1, depth), F32)),
        in_specs=[VMEM],
        out_specs=[VMEM] * 3,
        compiler_params=params(8),
        cost_estimate=cost(1),
        name="place_heads",
    )(parts)


def body(
    resid_in,
    queries,
    keys_in,
    value_rows_input,
    w_out,
    norm_gain,
    w_gate,
    w_up,
    w_down,
    cotangent,
    positions,
    doc_ids,
):
    rows = queries.shape[0]
    heads = queries.shape[1] // HEAD_WIDTH
    n_c, n_f = lax.axis_size("ctx"), lax.axis_size("ffn")
    c, f = lax.axis_index("ctx"), lax.axis_index("ffn")
    share, half = rows // n_f, n_f // 2
    depth = resid_in.shape[1]
    hidden_units = w_gate.shape[1]
    group = f * heads // (QUERY_HEADS // KEY_VALUE_HEADS)
    gain_row = norm_gain.reshape(1, depth)

    def exchange(x, axis, k):
        return lax.ppermute(x, axis, [(i, i ^ k) for i in range(lax.axis_size(axis))])

    def gather_rows(x):
        return jnp.concatenate([x] + [exchange(x, "ffn", 2 * m) for m in range(1, half)], axis=0)

    def beside(x):
        return exchange(x, "ffn", 1)

    def pair_sum(keep, give):
        return (keep.astype(F32) + beside(give).astype(F32)).astype(BF16)

    def scatter_rows(total):
        blocks = [total[m * share : (m + 1) * share] for m in range(half)]
        return [blocks[0]] + [exchange(blocks[m], "ffn", 2 * m) for m in range(1, half)]

    def after(x, *earlier):
        return lax.optimization_barrier((x, earlier))[0]

    bits = range(log2(n_c))

    def to_columns(blocks):
        return [blocks[0]] + [exchange(blocks[k], "ctx", k) for k in range(1, n_c)]

    cols = depth // n_c
    width = heads * HEAD_WIDTH
    pair = rows // 2
    f_ref = f.astype(jnp.int32).reshape(1)
    c_ref = c.astype(jnp.int32).reshape(1)
    q_rel, payload = prepare_call(
        f_ref,
        group.astype(jnp.int32).reshape(1),
        queries,
        keys_in,
        value_rows_input,
        positions.reshape(1, -1),
        doc_ids.reshape(1, -1),
        n_f,
    )
    pieces = [payload] + [exchange(payload, "ctx", k) for k in range(1, n_c)]
    cot_a = gather_rows(cotangent)
    cot_b = beside(cot_a)

    keep, give, att, lse = attention_call(f_ref, q_rel, w_out, pieces, n_f)
    terms = scatter_rows(pair_sum(keep, give))

    assert 2 * width == cols
    cot_blocks = list(column_blocks(c_ref, cot_a, n_c))
    att_blocks = [jnp.concatenate([att[:pair], att[pair:]], axis=1)]

    def crossing(bit):
        moving = [k for k in range(n_c) if k >> bit & 1]
        return moving, jnp.concatenate([cot_blocks[k] for k in moving] + att_blocks, axis=0)

    def crossed(moving, message):
        parts = [message[i : i + pair] for i in range(0, message.shape[0], pair)]
        for k, part in zip(moving, parts):
            cot_blocks[k] = part
        att_blocks.extend(parts[len(moving) :])

    moving, message = crossing(0)
    terms[0] = after(terms[0], message)
    hidden, normed = norm_call(resid_in, gain_row, terms)
    crossed(moving, exchange(message, "ctx", 1))

    grad_act = dot(jnp.concatenate([cot_a, cot_b], axis=0), w_down, NT)
    normed_a = gather_rows(normed)
    for bit in bits[1:]:
        moving, message = crossing(bit)
        if bit == bits[-1]:
            normed_a = after(normed_a, grad_act, message)
        crossed(moving, exchange(message, "ctx", 1 << bit))
    normed_b = beside(normed_a)
    normed_cols = to_columns(column_blocks(c_ref, normed_a, n_c))

    pay = gate_up_call(normed_a, normed_b, w_gate, w_up, grad_act)
    keep, give = normed_grad_call(pay, w_gate, w_up)
    normed_cols = jnp.concatenate(normed_cols, axis=0)
    give = after(give, normed_cols)
    total = pair_sum(keep, give)
    terms = scatter_rows(total)
    normed_side = beside(after(normed_cols, total))
    cot_cols = after(jnp.concatenate(cot_blocks, axis=0), total)
    cot_side = beside(cot_cols)

    late = after(pay, total)
    first, second = late[:pair], late[pair:]
    for bit in bits:
        first = jnp.concatenate([first, exchange(first, "ctx", 1 << bit)], axis=0)
        second = jnp.concatenate([second, exchange(second, "ctx", n_c >> 1 >> bit)], axis=0)
        if bit == bits[-2]:
            down = dot(after(pay, total)[:, :hidden_units], w_down).astype(BF16)
            terms[0] = after(terms[0], first, second, down)
            grad_resid, gain_part = norm_grad_call(cotangent, hidden, gain_row, terms)
            first, second = after((first, second), grad_resid)

    grad_a = gather_rows(grad_resid)
    down_total = pair_sum(down[:pair], down[pair:])
    grad_a = after(grad_a, down_total)
    grad_b = beside(grad_a)
    mixed_terms = scatter_rows(after(down_total, grad_a))

    grad_queries, *parts = attention_grad_call(
        f_ref, q_rel, att, lse, gain_part, grad_a, grad_b, w_out, pieces, n_f
    )
    parts = [parts[0]] + [exchange(parts[k], "ctx", k) for k in range(1, n_c)]
    grad_cols = to_columns(column_blocks(c_ref, after(grad_a, parts[1]), n_c))
    grad_cols = jnp.concatenate(grad_cols, axis=0)
    grad_side = beside(grad_cols)

    first, second = after((first, second), parts[0])
    reversed_bits = [sum((k >> b & 1) << (len(bits) - 1 - b) for b in bits) for k in range(n_c)]

    def hidden_part(i):
        at = i * hidden_units
        return [(0, 0, n_c * pair, at)] + [(1, k * pair, pair, at) for k in reversed_bits]

    columns = [(0, 0, n_c * pair, 0), (1, 0, n_c * pair, 0)]
    att_rows = [(k, 0, pair, 0) for k in range(n_c)] + [(k, 0, pair, width) for k in range(n_c)]
    normed_pair, shape = (normed_cols, normed_side), (cols, hidden_units)
    both = (first, second)
    grad_w_gate = weight_grad_call(columns, normed_pair, hidden_part(1), both, shape, "grad_w_gate")
    grad_w_up = weight_grad_call(columns, normed_pair, hidden_part(2), both, shape, "grad_w_up")
    grad_w_down = weight_grad_call(
        hidden_part(0), both, columns, (cot_cols, cot_side), (hidden_units, cols), "grad_w_down"
    )
    grad_w_out = weight_grad_call(
        att_rows, att_blocks, columns, (grad_cols, grad_side), (width, cols), "grad_w_out"
    )

    mixed = functools.reduce(jnp.add, [t.astype(F32) for t in mixed_terms])
    mixed = (hidden.astype(F32) + mixed).astype(BF16)

    grad_keys, grad_values, grad_gain = heads_call(
        lax.all_to_all(sum_call(parts, rows, n_f), "ffn", 0, 0), depth, n_f
    )
    return (
        mixed,
        grad_resid,
        grad_queries,
        grad_keys,
        grad_values,
        grad_gain.reshape(depth),
        grad_w_out,
        grad_w_gate,
        grad_w_up,
        grad_w_down,
    )


def solution(mesh):
    return jax.shard_map(
        body,
        mesh=mesh,
        in_specs=(
            P(("ctx", "ffn"), None),
            P("ctx", "ffn"),
            P("ctx", None),
            P("ctx", None),
            P("ffn", None),
            P(),
            P(None, "ffn"),
            P(None, "ffn"),
            P("ffn", None),
            P(("ctx", "ffn"), None),
            P("ctx"),
            P(),
        ),
        out_specs=(
            P(("ctx", "ffn"), None),
            P(("ctx", "ffn"), None),
            P("ctx", "ffn"),
            P(("ctx", "ffn"), None),
            P(("ctx", "ffn"), None),
            P(),
            P("ffn", "ctx"),
            P("ctx", "ffn"),
            P("ctx", "ffn"),
            P("ffn", "ctx"),
        ),
        check_vma=False,
    )
```

```python
import functools
import math

import jax
import jax.numpy as jnp
from jax import lax
from jax.experimental import pallas as pl
from jax.experimental.pallas import tpu as pltpu
from jax.sharding import PartitionSpec as P

QUERY_HEADS = 32
KEY_VALUE_HEADS = 8
HEAD_WIDTH = 128
STRIPE = 64

masked_fill = -1e30
norm_eps = 1e-05
score_scale = 1.0 / math.sqrt(HEAD_WIDTH)

F32 = jnp.float32
BF16 = jnp.bfloat16
NN = (((1,), (0,)), ((), ()))
NT = (((1,), (1,)), ((), ()))
TN = (((0,), (0,)), ((), ()))
VMEM = pl.BlockSpec(memory_space=pltpu.VMEM)
SMEM = pl.BlockSpec(memory_space=pltpu.SMEM)
ANY = pl.BlockSpec(memory_space=pl.ANY)


def dot(a, b, dims=NN):
    return lax.dot_general(a, b, dims, preferred_element_type=F32)


def params(megabytes=48):
    return pltpu.CompilerParams(vmem_limit_bytes=megabytes * 1024 * 1024)


def cost(microseconds):
    return pl.CostEstimate(
        flops=int(microseconds * 5e8), bytes_accessed=int(microseconds * 2e6), transcendentals=0
    )


def fetch(sources, targets, sems):
    copies = [pltpu.make_async_copy(s, t, sems.at[i]) for i, (s, t) in enumerate(zip(sources, targets))]
    for copy in copies:
        copy.start()
    return copies


def scratch_like(*arrays):
    return [pltpu.VMEM(a.shape, a.dtype) for a in arrays] + [
        pltpu.SemaphoreType.DMA((len(arrays),))
    ]


def log2(n):
    assert n & (n - 1) == 0
    return n.bit_length() - 1


def relative_rows(f, rows, n_f):
    share, half = rows // n_f, n_f // 2
    r = lax.broadcasted_iota(jnp.int32, (rows, rows), 0)
    natural = lax.broadcasted_iota(jnp.int32, (rows, rows), 1)
    j = lax.shift_right_logical(r, log2(share))
    k = lax.shift_left(j & (half - 1), 1) | lax.shift_right_logical(j, log2(half))
    return natural == lax.shift_left(k ^ f, log2(share)) + (r & (share - 1))


def visibility(same_row, pieces, rows):
    coded = [piece[2 * rows :, :].astype(F32) for piece in pieces]
    key_pos = jnp.concatenate([t[0:1] * STRIPE + t[1:2] for t in coded], axis=1)
    key_seg = jnp.concatenate([t[2:3] for t in coded], axis=1)

    def to_column(row):
        return jnp.sum(jnp.where(same_row, row[:, :rows], 0.0), axis=1, keepdims=True)

    return (key_pos <= to_column(key_pos)) & (key_seg == to_column(key_seg))


def keys_and_values(pieces, rows):
    return (
        jnp.concatenate([p[:rows] for p in pieces], axis=0),
        jnp.concatenate([p[rows : 2 * rows] for p in pieces], axis=0),
    )


def prepare_kernel(
    n_f, f_ref, group_ref, q_hbm, k_hbm, v_hbm, pos_hbm, doc_hbm, q_out, payload, *scratch
):
    q_ref, pos_ref, doc_ref, sems = scratch
    rows = q_ref.shape[0]
    cols = pl.ds(pl.multiple_of(group_ref[0] * HEAD_WIDTH, HEAD_WIDTH), HEAD_WIDTH)
    copies = fetch(
        [pos_hbm, doc_hbm, q_hbm, k_hbm.at[:, cols], v_hbm.at[:, cols]],
        [pos_ref, doc_ref, q_ref, payload.at[pl.ds(0, rows)], payload.at[pl.ds(rows, rows)]],
        sems,
    )
    same_row = relative_rows(f_ref[0], rows, n_f)
    line = lax.broadcasted_iota(jnp.int32, (16, rows), 0)
    copies[0].wait()
    copies[1].wait()
    pos = pos_ref[...]
    total = doc_ref.shape[1]
    where_is = lax.broadcasted_iota(jnp.int32, (total, rows), 0) == pos
    docs = jnp.broadcast_to(doc_ref[...].astype(F32), (8, total)).astype(BF16)
    seg = dot(docs, where_is.astype(F32).astype(BF16))[0:1]
    high = lax.shift_right_logical(pos, log2(STRIPE))
    low = pos & (STRIPE - 1)
    coded = jnp.where(line == 0, high.astype(F32), jnp.where(line == 1, low.astype(F32), 0.0))
    payload[2 * rows :, :] = jnp.where(line == 2, seg, coded).astype(BF16)
    copies[2].wait()
    q_out[...] = dot(same_row.astype(F32).astype(BF16), q_ref[...]).astype(BF16)
    copies[3].wait()
    copies[4].wait()


def prepare_call(f, group, queries, keys_in, values_in, pos_row, doc_row, n_f):
    rows = queries.shape[0]
    assert rows == HEAD_WIDTH
    return pl.pallas_call(
        functools.partial(prepare_kernel, n_f),
        out_shape=(
            jax.ShapeDtypeStruct(queries.shape, BF16),
            jax.ShapeDtypeStruct((2 * rows + 16, HEAD_WIDTH), BF16),
        ),
        in_specs=[SMEM, SMEM] + [ANY] * 5,
        out_specs=[VMEM] * 2,
        scratch_shapes=scratch_like(queries, pos_row, doc_row)[:-1]
        + [pltpu.SemaphoreType.DMA((5,))],
        compiler_params=params(58),
        cost_estimate=cost(2),
        name="prepare_attention",
    )(f, group, queries, keys_in, values_in, pos_row, doc_row)


def attention_kernel(n_f, n_c, f_ref, *refs):
    sources, refs = refs[: n_c + 2], refs[n_c + 2 :]
    (keep_ref, give_ref, att_ref, lse_ref), scratch, sems = refs[:4], refs[4:-1], refs[-1]
    copies = fetch(sources, scratch, sems)
    q_ref, pieces, w_ref = scratch[0], scratch[1:-1], scratch[-1]
    for copy in copies[:-1]:
        copy.wait()
    rows, width = q_ref.shape
    same_row = relative_rows(f_ref[0], rows, n_f)
    visible = visibility(same_row, pieces, rows)
    keys, values = keys_and_values(pieces, rows)
    q = q_ref[...]
    lane = lax.broadcasted_iota(jnp.int32, (rows, HEAD_WIDTH), 1)
    log_totals = jnp.zeros((rows, HEAD_WIDTH), F32)
    for h in range(width // HEAD_WIDTH):
        cols = slice(h * HEAD_WIDTH, (h + 1) * HEAD_WIDTH)
        scores = jnp.where(visible, dot(q[:, cols], keys, NT) * score_scale, masked_fill)
        row_max = jnp.max(scores, axis=1, keepdims=True)
        weights = jnp.exp(scores - row_max)
        row_total = jnp.sum(weights, axis=1, keepdims=True)
        att_ref[:, cols] = (dot(weights.astype(BF16), values) / row_total).astype(BF16)
        log_totals = jnp.where(lane == h, row_max + jnp.log(row_total), log_totals)
    lse_ref[...] = log_totals
    copies[-1].wait()
    att = att_ref[...]
    tile = 512
    for start in range(0, w_ref.shape[1], tile):
        out = dot(att, w_ref[:, start : start + tile]).astype(BF16)
        keep_ref[:, start : start + tile] = out[: rows // 2]
        give_ref[:, start : start + tile] = out[rows // 2 :]


def attention_call(f, queries, w_out, pieces, n_f):
    rows, width = queries.shape
    depth = w_out.shape[1]
    half = jax.ShapeDtypeStruct((rows // 2, depth), BF16)
    att = jax.ShapeDtypeStruct((rows, width), BF16)
    lse = jax.ShapeDtypeStruct((rows, HEAD_WIDTH), F32)
    return pl.pallas_call(
        functools.partial(attention_kernel, n_f, len(pieces)),
        out_shape=(half, half, att, lse),
        in_specs=[SMEM] + [ANY] * (2 + len(pieces)),
        out_specs=[VMEM] * 4,
        scratch_shapes=scratch_like(queries, *pieces, w_out),
        compiler_params=params(56),
        cost_estimate=cost(4),
        name="attention_and_projection",
    )(f, queries, *pieces, w_out)


def fold(row):
    width = 2 * HEAD_WIDTH
    return [row[:, i : i + width] for i in range(0, row.shape[1], width)]


def attention_grad_kernel(n_f, n_c, f_ref, *refs):
    pieces, refs = refs[:n_c], refs[n_c:]
    q_ref, att_ref, lse_ref, gain_ref, ga_ref, gb_ref, w_ref = refs[:7]
    dq_ref, dkv_refs = refs[7], refs[8:]
    rows, width = q_ref.shape
    same_row = relative_rows(f_ref[0], rows, n_f)
    visible = visibility(same_row, pieces, rows)
    keys, values = keys_and_values(pieces, rows)
    order = same_row.astype(F32).astype(BF16)
    q = q_ref[...]
    grad_rows = jnp.concatenate([ga_ref[...], gb_ref[...]], axis=0)
    grad_att = dot(grad_rows, w_ref[...], NT).astype(BF16)
    grad_keys = jnp.zeros(keys.shape, F32)
    grad_values = jnp.zeros(keys.shape, F32)
    grad_q = []
    for h in range(width // HEAD_WIDTH):
        cols = slice(h * HEAD_WIDTH, (h + 1) * HEAD_WIDTH)
        g = grad_att[:, cols]
        scores = jnp.where(visible, dot(q[:, cols], keys, NT) * score_scale, masked_fill)
        probs = jnp.exp(scores - lse_ref[:, h : h + 1])
        delta = jnp.sum(g.astype(F32) * att_ref[:, cols].astype(F32), axis=1, keepdims=True)
        grad_scores = (probs * (dot(g, values, NT) - delta)).astype(BF16)
        grad_q.append((dot(grad_scores, keys) * score_scale).astype(BF16))
        grad_keys = grad_keys + dot(grad_scores, q[:, cols], TN)
        grad_values = grad_values + dot(probs.astype(BF16), g, TN)
    dq_ref[...] = dot(order, jnp.concatenate(grad_q, axis=1), TN).astype(BF16)
    high = gain_ref[...].astype(BF16)
    low = (gain_ref[...] - high.astype(F32)).astype(BF16)
    lines = fold(high) + fold(low)
    for k, dkv_ref in enumerate(dkv_refs):
        part = slice(k * rows, (k + 1) * rows)
        dkv_ref[:rows, :HEAD_WIDTH] = (grad_keys[part] * score_scale).astype(BF16)
        dkv_ref[:rows, HEAD_WIDTH:] = grad_values[part].astype(BF16)
        for i, line in enumerate(lines):
            dkv_ref[rows + i : rows + i + 1, :] = line


def attention_grad_call(f, queries, att, lse, gain, grad_a, grad_b, w_out, pieces, n_f):
    rows, width = queries.shape
    n_c = len(pieces)
    dkv = jax.ShapeDtypeStruct((rows + gain.shape[1] // HEAD_WIDTH, 2 * HEAD_WIDTH), BF16)
    return pl.pallas_call(
        functools.partial(attention_grad_kernel, n_f, n_c),
        out_shape=(jax.ShapeDtypeStruct((rows, width), BF16),) + (dkv,) * n_c,
        in_specs=[SMEM] + [VMEM] * (7 + n_c),
        out_specs=(VMEM,) * (1 + n_c),
        compiler_params=params(24),
        cost_estimate=cost(4),
        name="attention_gradients",
    )(f, *pieces, queries, att, lse, gain, grad_a, grad_b, w_out)


def norm_kernel(resid_ref, gain_ref, *refs):
    terms, (hidden_ref, normed_ref) = refs[:-2], refs[-2:]
    total = resid_ref[...].astype(F32)
    total = total + functools.reduce(jnp.add, [t[...].astype(F32) for t in terms])
    hidden = total.astype(BF16)
    hidden_ref[...] = hidden
    hidden = hidden.astype(F32)
    inv_rms = lax.rsqrt(jnp.mean(hidden * hidden, axis=1, keepdims=True) + norm_eps)
    normed_ref[...] = (hidden * inv_rms * gain_ref[...]).astype(BF16)


def norm_call(resid, gain_row, terms):
    out = jax.ShapeDtypeStruct(resid.shape, BF16)
    return pl.pallas_call(
        norm_kernel,
        out_shape=(out, out),
        in_specs=[VMEM] * (2 + len(terms)),
        out_specs=[VMEM] * 2,
        compiler_params=params(8),
        cost_estimate=cost(8),
        name="residual_and_norm",
    )(resid, gain_row, *terms)


def norm_grad_kernel(cot_ref, hidden_ref, gain_ref, *refs):
    terms, (grad_ref, gain_grad_ref) = refs[:-2], refs[-2:]
    grad_normed = functools.reduce(jnp.add, [t[...].astype(F32) for t in terms])
    hidden = hidden_ref[...].astype(F32)
    inv_rms = lax.rsqrt(jnp.mean(hidden * hidden, axis=1, keepdims=True) + norm_eps)
    gained = grad_normed * gain_ref[...]
    inv_cube = inv_rms * inv_rms * inv_rms
    grad_ref[...] = (
        cot_ref[...].astype(F32)
        + inv_rms * gained
        - hidden * inv_cube * jnp.mean(gained * hidden, axis=1, keepdims=True)
    ).astype(BF16)
    gain_grad_ref[...] = jnp.sum(grad_normed * hidden * inv_rms, axis=0, keepdims=True)


def norm_grad_call(cot, hidden, gain_row, terms):
    return pl.pallas_call(
        norm_grad_kernel,
        out_shape=(
            jax.ShapeDtypeStruct(cot.shape, BF16),
            jax.ShapeDtypeStruct(gain_row.shape, F32),
        ),
        in_specs=[VMEM] * (3 + len(terms)),
        out_specs=[VMEM] * 2,
        compiler_params=params(8),
        cost_estimate=cost(8),
        name="norm_gradients",
    )(cot, hidden, gain_row, *terms)


def gate_up_kernel(xa_ref, xb_ref, wg_ref, wu_ref, ga_ref, out_ref, gate_acc, up_acc):
    depth, width = wg_ref.shape
    half = xa_ref.shape[0]
    tile = 512
    gate_acc[...] = jnp.zeros_like(gate_acc)
    up_acc[...] = jnp.zeros_like(up_acc)

    @pl.loop(0, depth // tile)
    def _(step):
        at = pl.ds(pl.multiple_of(step * tile, tile), tile)
        x = jnp.concatenate([xa_ref[:, at], xb_ref[:, at]], axis=0)
        gate_acc[...] += dot(x, wg_ref[at, :])
        up_acc[...] += dot(x, wu_ref[at, :])

    gate, up, grad_act = gate_acc[...], up_acc[...], ga_ref[...]
    sig = jax.nn.sigmoid(gate)
    out_ref[:, :width] = (gate * sig * up).astype(BF16)
    out_ref[:, width : 2 * width] = (grad_act * up * sig * (1.0 + gate * (1.0 - sig))).astype(BF16)
    out_ref[:, 2 * width :] = (grad_act * gate * sig).astype(BF16)


def gate_up_call(xa, xb, w_gate, w_up, grad_act):
    depth, width = w_gate.shape
    rows = grad_act.shape[0]
    return pl.pallas_call(
        gate_up_kernel,
        out_shape=jax.ShapeDtypeStruct((rows, 3 * width), BF16),
        in_specs=[VMEM] * 5,
        out_specs=VMEM,
        scratch_shapes=[pltpu.VMEM((rows, width), F32)] * 2,
        compiler_params=params(24),
        cost_estimate=cost(2),
        name="gate_up_and_gradients",
    )(xa, xb, w_gate, w_up, grad_act)


def normed_grad_kernel(pay_ref, wg_ref, wu_ref, keep_ref, give_ref):
    depth, width = wg_ref.shape
    half = keep_ref.shape[0]
    tile = 512

    @pl.loop(0, depth // tile)
    def _(step):
        at = pl.ds(pl.multiple_of(step * tile, tile), tile)
        out = dot(pay_ref[:, width : 2 * width], wg_ref[at, :], NT)
        out = (out + dot(pay_ref[:, 2 * width :], wu_ref[at, :], NT)).astype(BF16)
        keep_ref[:, at] = out[:half]
        give_ref[:, at] = out[half:]


def normed_grad_call(pay, w_gate, w_up):
    depth, width = w_gate.shape
    rows = pay.shape[0]
    out = jax.ShapeDtypeStruct((rows // 2, depth), BF16)
    return pl.pallas_call(
        normed_grad_kernel,
        out_shape=(out, out),
        in_specs=[VMEM] * 3,
        out_specs=[VMEM] * 2,
        compiler_params=params(24),
        cost_estimate=cost(2),
        name="normed_gradients",
    )(pay, w_gate, w_up)


def column_blocks_kernel(c_ref, a_ref, *out_refs):
    cols = a_ref.shape[1] // len(out_refs)
    for k, out_ref in enumerate(out_refs):
        start = pl.multiple_of((c_ref[0] ^ k) * cols, 128)
        out_ref[...] = a_ref[:, pl.ds(start, cols)]


def column_blocks(c, a, n_c):
    rows, depth = a.shape
    return pl.pallas_call(
        column_blocks_kernel,
        out_shape=(jax.ShapeDtypeStruct((rows, depth // n_c), BF16),) * n_c,
        in_specs=[SMEM, VMEM],
        out_specs=(VMEM,) * n_c,
        compiler_params=params(8),
        cost_estimate=cost(1),
        name="column_blocks",
    )(c, a)


def take(refs, pieces, width):
    return jnp.concatenate([refs[i][r : r + n, at : at + width] for i, r, n, at in pieces], axis=0)


def weight_grad_kernel(left, right, n_left, widths, *refs):
    out_ref = refs[-1]
    rhs = take(refs[n_left:-1], right, widths[1])
    tile = 256
    for at in range(0, widths[0], tile):
        size = min(tile, widths[0] - at)
        lhs = take(refs[:n_left], [(i, r, n, first + at) for i, r, n, first in left], size)
        out_ref[at : at + size, :] = dot(lhs, rhs, TN)


def weight_grad_call(left, left_refs, right, right_refs, widths, name):
    return pl.pallas_call(
        functools.partial(weight_grad_kernel, left, right, len(left_refs), widths),
        out_shape=jax.ShapeDtypeStruct(widths, F32),
        in_specs=[VMEM] * (len(left_refs) + len(right_refs)),
        out_specs=VMEM,
        compiler_params=params(16),
        cost_estimate=cost(4),
        name=name,
    )(*left_refs, *right_refs)


def tree_sum(values):
    while len(values) > 1:
        values = [values[i] + values[i + 1] for i in range(0, len(values), 2)]
    return values[0]


def sum_kernel(n_f, rows, f_ref, *refs):
    parts, (own_ref, beside_ref, total_ref) = refs[:-3], refs[-3:]
    share, lines = rows // n_f, (parts[0].shape[0] - rows) // 2
    total_ref[...] = tree_sum([p[:rows, :].astype(F32) for p in parts])
    gain = tree_sum(
        [p[rows : rows + lines, :].astype(F32) + p[rows + lines :, :].astype(F32) for p in parts]
    )
    high = gain.astype(BF16)
    low = (gain - high.astype(F32)).astype(BF16)
    for k in range(n_f):
        out_ref = (own_ref, beside_ref)[k % 2]
        start = pl.multiple_of((f_ref[0] ^ k) * share, share)
        out_ref[k // 2, :lines, :] = high
        out_ref[k // 2, lines : 2 * lines, :] = low
        out_ref[k // 2, 2 * lines :, :] = total_ref[pl.ds(start, share), :].astype(BF16)


def sum_call(f, parts, rows, n_f):
    lines = parts[0].shape[0] - rows
    out = jax.ShapeDtypeStruct((n_f // 2, lines + rows // n_f, 2 * HEAD_WIDTH), BF16)
    return pl.pallas_call(
        functools.partial(sum_kernel, n_f, rows),
        out_shape=(out, out),
        in_specs=[SMEM] + [VMEM] * len(parts),
        out_specs=(VMEM, VMEM),
        scratch_shapes=[pltpu.VMEM((rows, 2 * HEAD_WIDTH), F32)],
        compiler_params=params(8),
        cost_estimate=cost(1),
        name="sum_over_ctx",
    )(f, *parts)


def heads_kernel(n_f, f_ref, *refs):
    in_refs, (dk_ref, dv_ref, gain_ref) = refs[:-3], refs[-3:]
    per_head = n_f // KEY_VALUE_HEADS
    width = 2 * HEAD_WIDTH
    lines = gain_ref.shape[1] // width
    chunks = [(ref, i) for ref in in_refs for i in range(2)]
    for k in range(0, n_f, per_head):
        total = tree_sum([r[i, 2 * lines :, :].astype(F32) for r, i in chunks[k : k + per_head]])
        head = lax.shift_right_logical(f_ref[0] ^ k, log2(per_head))
        at = pl.ds(pl.multiple_of(head * HEAD_WIDTH, HEAD_WIDTH), HEAD_WIDTH)
        dk_ref[:, at] = total[:, :HEAD_WIDTH]
        dv_ref[:, at] = total[:, HEAD_WIDTH:]
    gain = tree_sum(
        [
            r[i, :lines, :].astype(F32) + r[i, lines : 2 * lines, :].astype(F32)
            for r, i in chunks
        ]
    )
    for i in range(lines):
        gain_ref[:, i * width : (i + 1) * width] = gain[i : i + 1]


def heads_call(f, pairs, depth, n_f):
    share = pairs[0].shape[1] - depth // HEAD_WIDTH
    out = jax.ShapeDtypeStruct((share, KEY_VALUE_HEADS * HEAD_WIDTH), F32)
    return pl.pallas_call(
        functools.partial(heads_kernel, n_f),
        out_shape=(out, out, jax.ShapeDtypeStruct((1, depth), F32)),
        in_specs=[SMEM] + [VMEM] * len(pairs),
        out_specs=[VMEM] * 3,
        compiler_params=params(8),
        cost_estimate=cost(1),
        name="place_heads",
    )(f, *pairs)


def body(
    resid_in,
    queries,
    keys_in,
    value_rows_input,
    w_out,
    norm_gain,
    w_gate,
    w_up,
    w_down,
    cotangent,
    positions,
    doc_ids,
):
    rows = queries.shape[0]
    heads = queries.shape[1] // HEAD_WIDTH
    n_c, n_f = lax.axis_size("ctx"), lax.axis_size("ffn")
    c, f = lax.axis_index("ctx"), lax.axis_index("ffn")
    share, half = rows // n_f, n_f // 2
    depth = resid_in.shape[1]
    hidden_units = w_gate.shape[1]
    group = f * heads // (QUERY_HEADS // KEY_VALUE_HEADS)
    gain_row = norm_gain.reshape(1, depth)

    def exchange(x, axis, k):
        return lax.ppermute(x, axis, [(i, i ^ k) for i in range(lax.axis_size(axis))])

    def gather_rows(x):
        return jnp.concatenate([x] + [exchange(x, "ffn", 2 * m) for m in range(1, half)], axis=0)

    def beside(x):
        return exchange(x, "ffn", 1)

    def pair_sum(keep, give):
        return (keep.astype(F32) + beside(give).astype(F32)).astype(BF16)

    def scatter_rows(total):
        blocks = [total[m * share : (m + 1) * share] for m in range(half)]
        return [blocks[0]] + [exchange(blocks[m], "ffn", 2 * m) for m in range(1, half)]

    def after(x, *earlier):
        return lax.optimization_barrier((x, earlier))[0]

    bits = range(log2(n_c))

    def to_columns(blocks):
        return [blocks[0]] + [exchange(blocks[k], "ctx", k) for k in range(1, n_c)]

    cols = depth // n_c
    width = heads * HEAD_WIDTH
    pair = rows // 2
    f_ref = f.astype(jnp.int32).reshape(1)
    c_ref = c.astype(jnp.int32).reshape(1)
    q_rel, payload = prepare_call(
        f_ref,
        group.astype(jnp.int32).reshape(1),
        queries,
        keys_in,
        value_rows_input,
        positions.reshape(1, -1),
        doc_ids.reshape(1, -1),
        n_f,
    )
    pieces = [payload] + [exchange(payload, "ctx", k) for k in range(1, n_c)]
    cot_a = gather_rows(cotangent)

    keep, give, att, lse = attention_call(f_ref, q_rel, w_out, pieces, n_f)
    terms = scatter_rows(pair_sum(keep, give))

    assert 2 * width == cols
    cot_late = after(cot_a, terms[1])
    cot_b = beside(cot_late)
    cot_blocks = list(column_blocks(c_ref, cot_late, n_c))
    att_blocks = [jnp.concatenate([att[:pair], att[pair:]], axis=1)]

    def crossing(bit):
        moving = [k for k in range(n_c) if k >> bit & 1]
        return moving, jnp.concatenate([cot_blocks[k] for k in moving] + att_blocks, axis=0)

    def crossed(moving, message):
        parts = [message[i : i + pair] for i in range(0, message.shape[0], pair)]
        for k, part in zip(moving, parts):
            cot_blocks[k] = part
        att_blocks.extend(parts[len(moving) :])

    hidden, normed = norm_call(resid_in, gain_row, terms)
    normed_a = gather_rows(normed)
    for bit in bits:
        moving, message = crossing(bit)
        if bit == bits[-1]:
            grad_act = dot(jnp.concatenate([cot_late, cot_b], axis=0), w_down, NT)
            normed_a = after(normed_a, grad_act, message)
        crossed(moving, exchange(message, "ctx", 1 << bit))
    normed_b = beside(normed_a)

    pay = gate_up_call(normed_a, normed_b, w_gate, w_up, grad_act)
    keep, give = normed_grad_call(pay, w_gate, w_up)
    total = pair_sum(keep, give)
    terms = scatter_rows(total)
    cot_cols = after(jnp.concatenate(cot_blocks, axis=0), total)
    cot_side = beside(cot_cols)

    late, normed_late = after((pay, normed_a), total)
    normed_blocks = column_blocks(c_ref, normed_late, n_c)

    class Half:
        def __init__(self, side):
            self.side = side
            self.order = list(bits) if side == 0 else list(bits)[::-1]
            lanes = slice(side * cols // 2, (side + 1) * cols // 2)
            self.columns = [block[:, lanes] for block in normed_blocks]
            self.arrays = [late]
            self.rows = {0: (0, side * pair, 0)}

        def row(self, k):
            array, start, at = self.rows[k]
            return self.arrays[array][start : start + pair, at : at + 3 * hidden_units]

        def message(self, step):
            bit = self.order[step]
            self.held = list(self.rows)
            self.moving = [k for k in range(n_c) if k >> bit & 1]
            parts = [self.row(k) for k in self.held] + [self.columns[k] for k in self.moving]
            return jnp.concatenate(parts, axis=1)

        def send(self, step, message):
            bit = self.order[step]
            self.arrays.append(exchange(message, "ctx", 1 << bit))
            at = 0
            for k in self.held:
                self.rows[k | 1 << bit] = (len(self.arrays) - 1, 0, at)
                at += 3 * hidden_units
            for k in self.moving:
                self.columns[k] = self.arrays[-1][:, at : at + cols // 2]
                at += cols // 2

    halves = [Half(0), Half(1)]
    for step in bits:
        messages = [h.message(step) for h in halves]
        if step == bits[-1]:
            down = dot(late[:, :hidden_units], w_down).astype(BF16)
            terms[0] = after(terms[0], messages[0], messages[1], down)
            grad_resid, gain_part = norm_grad_call(cotangent, hidden, gain_row, terms)
        for h, message in zip(halves, messages):
            h.send(step, message)

    grad_a = gather_rows(grad_resid)
    down_total = pair_sum(down[:pair], down[pair:])
    grad_a = after(grad_a, down_total)
    grad_b = beside(grad_a)
    mixed_terms = scatter_rows(after(down_total, grad_a))

    grad_queries, *parts = attention_grad_call(
        f_ref, q_rel, att, lse, gain_part, grad_a, grad_b, w_out, pieces, n_f
    )
    parts = [parts[0]] + [exchange(parts[k], "ctx", k) for k in range(1, n_c)]
    grad_cols = to_columns(column_blocks(c_ref, after(grad_a, *parts), n_c))
    grad_cols = jnp.concatenate(grad_cols, axis=0)
    grad_side = beside(grad_cols)

    own_chunks, beside_chunks = sum_call(f_ref, parts, rows, n_f)
    chunks = jnp.stack([own_chunks, beside(beside_chunks)], axis=1)
    chunks = [chunks[0]] + [exchange(chunks[m], "ffn", 2 * m) for m in range(1, half)]
    grad_keys, grad_values, grad_gain = heads_call(f_ref, chunks, depth, n_f)

    normed_cols = jnp.concatenate(
        [jnp.concatenate([h.columns[k] for h in halves], axis=1) for k in range(n_c)], axis=0
    )
    normed_cols = after(normed_cols, parts[0])
    normed_side = beside(normed_cols)
    offset = len(halves[0].arrays)
    hidden_refs = halves[0].arrays + halves[1].arrays

    def hidden_part(i):
        pieces = []
        for side, h in enumerate(halves):
            for k in range(n_c):
                array, start, at = h.rows[k]
                pieces.append((array + side * offset, start, pair, at + i * hidden_units))
        return pieces

    columns = [(0, 0, n_c * pair, 0), (1, 0, n_c * pair, 0)]
    att_rows = [(k, 0, pair, 0) for k in range(n_c)] + [(k, 0, pair, width) for k in range(n_c)]
    normed_pair, shape = (normed_cols, normed_side), (cols, hidden_units)
    grad_w_gate = weight_grad_call(
        columns, normed_pair, hidden_part(1), hidden_refs, shape, "grad_w_gate"
    )
    grad_w_up = weight_grad_call(
        columns, normed_pair, hidden_part(2), hidden_refs, shape, "grad_w_up"
    )
    grad_w_down = weight_grad_call(
        hidden_part(0), hidden_refs, columns, (cot_cols, cot_side), shape[::-1], "grad_w_down"
    )
    grad_w_out = weight_grad_call(
        att_rows, att_blocks, columns, (grad_cols, grad_side), (width, cols), "grad_w_out"
    )

    mixed = functools.reduce(jnp.add, [t.astype(F32) for t in mixed_terms])
    mixed = (hidden.astype(F32) + mixed).astype(BF16)

    return (
        mixed,
        grad_resid,
        grad_queries,
        grad_keys,
        grad_values,
        grad_gain.reshape(depth),
        grad_w_out,
        grad_w_gate,
        grad_w_up,
        grad_w_down,
    )


def solution(mesh):
    return jax.shard_map(
        body,
        mesh=mesh,
        in_specs=(
            P(("ctx", "ffn"), None),
            P("ctx", "ffn"),
            P("ctx", None),
            P("ctx", None),
            P("ffn", None),
            P(),
            P(None, "ffn"),
            P(None, "ffn"),
            P("ffn", None),
            P(("ctx", "ffn"), None),
            P("ctx"),
            P(),
        ),
        out_specs=(
            P(("ctx", "ffn"), None),
            P(("ctx", "ffn"), None),
            P("ctx", "ffn"),
            P(("ctx", "ffn"), None),
            P(("ctx", "ffn"), None),
            P(),
            P("ffn", "ctx"),
            P("ctx", "ffn"),
            P("ctx", "ffn"),
            P("ffn", "ctx"),
        ),
        check_vma=False,
    )
```

```python
import functools
import math

import jax
import jax.numpy as jnp
from jax import lax
from jax.experimental import pallas as pl
from jax.experimental.pallas import tpu as pltpu
from jax.sharding import PartitionSpec as P

QUERY_HEADS = 32
KEY_VALUE_HEADS = 8
HEAD_WIDTH = 128
STRIPE = 64

masked_fill = -1e30
norm_eps = 1e-05
score_scale = 1.0 / math.sqrt(HEAD_WIDTH)

F32 = jnp.float32
BF16 = jnp.bfloat16
NN = (((1,), (0,)), ((), ()))
NT = (((1,), (1,)), ((), ()))
TN = (((0,), (0,)), ((), ()))
VMEM = pl.BlockSpec(memory_space=pltpu.VMEM)
SMEM = pl.BlockSpec(memory_space=pltpu.SMEM)
ANY = pl.BlockSpec(memory_space=pl.ANY)


def dot(a, b, dims=NN):
    return lax.dot_general(a, b, dims, preferred_element_type=F32)


def params(megabytes=48):
    return pltpu.CompilerParams(vmem_limit_bytes=megabytes * 1024 * 1024)


def cost(microseconds):
    return pl.CostEstimate(
        flops=int(microseconds * 5e8), bytes_accessed=int(microseconds * 2e6), transcendentals=0
    )


def fetch(sources, targets, sems):
    copies = [pltpu.make_async_copy(s, t, sems.at[i]) for i, (s, t) in enumerate(zip(sources, targets))]
    for copy in copies:
        copy.start()
    return copies


def scratch_like(*arrays):
    return [pltpu.VMEM(a.shape, a.dtype) for a in arrays] + [
        pltpu.SemaphoreType.DMA((len(arrays),))
    ]


def log2(n):
    assert n & (n - 1) == 0
    return n.bit_length() - 1


def relative_rows(f, rows, n_f):
    share, half = rows // n_f, n_f // 2
    r = lax.broadcasted_iota(jnp.int32, (rows, rows), 0)
    natural = lax.broadcasted_iota(jnp.int32, (rows, rows), 1)
    j = lax.shift_right_logical(r, log2(share))
    k = lax.shift_left(j & (half - 1), 1) | lax.shift_right_logical(j, log2(half))
    return natural == lax.shift_left(k ^ f, log2(share)) + (r & (share - 1))


def visibility(same_row, pieces, rows):
    coded = [piece[2 * rows :, :].astype(F32) for piece in pieces]
    key_pos = jnp.concatenate([t[0:1] * STRIPE + t[1:2] for t in coded], axis=1)
    key_seg = jnp.concatenate([t[2:3] for t in coded], axis=1)

    def to_column(row):
        return jnp.sum(jnp.where(same_row, row[:, :rows], 0.0), axis=1, keepdims=True)

    return (key_pos <= to_column(key_pos)) & (key_seg == to_column(key_seg))


def keys_and_values(pieces, rows):
    return (
        jnp.concatenate([p[:rows] for p in pieces], axis=0),
        jnp.concatenate([p[rows : 2 * rows] for p in pieces], axis=0),
    )


def prepare_kernel(
    n_f, f_ref, group_ref, q_hbm, k_hbm, v_hbm, pos_hbm, doc_hbm, q_out, payload, *scratch
):
    q_ref, pos_ref, doc_ref, sems = scratch
    rows = q_ref.shape[0]
    cols = pl.ds(pl.multiple_of(group_ref[0] * HEAD_WIDTH, HEAD_WIDTH), HEAD_WIDTH)
    copies = fetch(
        [pos_hbm, doc_hbm, q_hbm, k_hbm.at[:, cols], v_hbm.at[:, cols]],
        [pos_ref, doc_ref, q_ref, payload.at[pl.ds(0, rows)], payload.at[pl.ds(rows, rows)]],
        sems,
    )
    same_row = relative_rows(f_ref[0], rows, n_f)
    line = lax.broadcasted_iota(jnp.int32, (16, rows), 0)
    copies[0].wait()
    copies[1].wait()
    pos = pos_ref[...]
    total = doc_ref.shape[1]
    where_is = lax.broadcasted_iota(jnp.int32, (total, rows), 0) == pos
    docs = jnp.broadcast_to(doc_ref[...].astype(F32), (8, total)).astype(BF16)
    seg = dot(docs, where_is.astype(F32).astype(BF16))[0:1]
    high = lax.shift_right_logical(pos, log2(STRIPE))
    low = pos & (STRIPE - 1)
    coded = jnp.where(line == 0, high.astype(F32), jnp.where(line == 1, low.astype(F32), 0.0))
    payload[2 * rows :, :] = jnp.where(line == 2, seg, coded).astype(BF16)
    copies[2].wait()
    q_out[...] = dot(same_row.astype(F32).astype(BF16), q_ref[...]).astype(BF16)
    copies[3].wait()
    copies[4].wait()


def prepare_call(f, group, queries, keys_in, values_in, pos_row, doc_row, n_f):
    rows = queries.shape[0]
    assert rows == HEAD_WIDTH
    return pl.pallas_call(
        functools.partial(prepare_kernel, n_f),
        out_shape=(
            jax.ShapeDtypeStruct(queries.shape, BF16),
            jax.ShapeDtypeStruct((2 * rows + 16, HEAD_WIDTH), BF16),
        ),
        in_specs=[SMEM, SMEM] + [ANY] * 5,
        out_specs=[VMEM] * 2,
        scratch_shapes=scratch_like(queries, pos_row, doc_row)[:-1]
        + [pltpu.SemaphoreType.DMA((5,))],
        compiler_params=params(58),
        cost_estimate=cost(2),
        name="prepare_attention",
    )(f, group, queries, keys_in, values_in, pos_row, doc_row)


def attention_kernel(n_f, n_c, f_ref, *refs):
    sources, refs = refs[: n_c + 2], refs[n_c + 2 :]
    (keep_ref, give_ref, att_ref, lse_ref), scratch, sems = refs[:4], refs[4:-1], refs[-1]
    copies = fetch(sources, scratch, sems)
    q_ref, pieces, w_ref = scratch[0], scratch[1:-1], scratch[-1]
    for copy in copies[:-1]:
        copy.wait()
    rows, width = q_ref.shape
    same_row = relative_rows(f_ref[0], rows, n_f)
    visible = visibility(same_row, pieces, rows)
    keys, values = keys_and_values(pieces, rows)
    q = q_ref[...]
    lane = lax.broadcasted_iota(jnp.int32, (rows, HEAD_WIDTH), 1)
    log_totals = jnp.zeros((rows, HEAD_WIDTH), F32)
    for h in range(width // HEAD_WIDTH):
        cols = slice(h * HEAD_WIDTH, (h + 1) * HEAD_WIDTH)
        scores = jnp.where(visible, dot(q[:, cols], keys, NT) * score_scale, masked_fill)
        row_max = jnp.max(scores, axis=1, keepdims=True)
        weights = jnp.exp(scores - row_max)
        row_total = jnp.sum(weights, axis=1, keepdims=True)
        att_ref[:, cols] = (dot(weights.astype(BF16), values) / row_total).astype(BF16)
        log_totals = jnp.where(lane == h, row_max + jnp.log(row_total), log_totals)
    lse_ref[...] = log_totals
    copies[-1].wait()
    att = att_ref[...]
    tile = 512
    for start in range(0, w_ref.shape[1], tile):
        out = dot(att, w_ref[:, start : start + tile]).astype(BF16)
        keep_ref[:, start : start + tile] = out[: rows // 2]
        give_ref[:, start : start + tile] = out[rows // 2 :]


def attention_call(f, queries, w_out, pieces, n_f):
    rows, width = queries.shape
    depth = w_out.shape[1]
    half = jax.ShapeDtypeStruct((rows // 2, depth), BF16)
    att = jax.ShapeDtypeStruct((rows, width), BF16)
    lse = jax.ShapeDtypeStruct((rows, HEAD_WIDTH), F32)
    return pl.pallas_call(
        functools.partial(attention_kernel, n_f, len(pieces)),
        out_shape=(half, half, att, lse),
        in_specs=[SMEM] + [ANY] * (2 + len(pieces)),
        out_specs=[VMEM] * 4,
        scratch_shapes=scratch_like(queries, *pieces, w_out),
        compiler_params=params(56),
        cost_estimate=cost(4),
        name="attention_and_projection",
    )(f, queries, *pieces, w_out)


def fold(row):
    width = 2 * HEAD_WIDTH
    return [row[:, i : i + width] for i in range(0, row.shape[1], width)]


def attention_grad_kernel(n_f, n_c, f_ref, *refs):
    pieces, refs = refs[:n_c], refs[n_c:]
    q_ref, att_ref, lse_ref, gain_ref, ga_ref, gb_ref, w_ref = refs[:7]
    dq_ref, dkv_refs = refs[7], refs[8:]
    rows, width = q_ref.shape
    same_row = relative_rows(f_ref[0], rows, n_f)
    visible = visibility(same_row, pieces, rows)
    keys, values = keys_and_values(pieces, rows)
    order = same_row.astype(F32).astype(BF16)
    q = q_ref[...]
    grad_rows = jnp.concatenate([ga_ref[...], gb_ref[...]], axis=0)
    grad_att = dot(grad_rows, w_ref[...], NT).astype(BF16)
    grad_keys = jnp.zeros(keys.shape, F32)
    grad_values = jnp.zeros(keys.shape, F32)
    grad_q = []
    for h in range(width // HEAD_WIDTH):
        cols = slice(h * HEAD_WIDTH, (h + 1) * HEAD_WIDTH)
        g = grad_att[:, cols]
        scores = jnp.where(visible, dot(q[:, cols], keys, NT) * score_scale, masked_fill)
        probs = jnp.exp(scores - lse_ref[:, h : h + 1])
        delta = jnp.sum(g.astype(F32) * att_ref[:, cols].astype(F32), axis=1, keepdims=True)
        grad_scores = (probs * (dot(g, values, NT) - delta)).astype(BF16)
        grad_q.append((dot(grad_scores, keys) * score_scale).astype(BF16))
        grad_keys = grad_keys + dot(grad_scores, q[:, cols], TN)
        grad_values = grad_values + dot(probs.astype(BF16), g, TN)
    dq_ref[...] = dot(order, jnp.concatenate(grad_q, axis=1), TN).astype(BF16)
    high = gain_ref[...].astype(BF16)
    low = (gain_ref[...] - high.astype(F32)).astype(BF16)
    lines = fold(high) + fold(low)
    for k, dkv_ref in enumerate(dkv_refs):
        part = slice(k * rows, (k + 1) * rows)
        dkv_ref[:rows, :HEAD_WIDTH] = (grad_keys[part] * score_scale).astype(BF16)
        dkv_ref[:rows, HEAD_WIDTH:] = grad_values[part].astype(BF16)
        for i, line in enumerate(lines):
            dkv_ref[rows + i : rows + i + 1, :] = line


def attention_grad_call(f, queries, att, lse, gain, grad_a, grad_b, w_out, pieces, n_f):
    rows, width = queries.shape
    n_c = len(pieces)
    dkv = jax.ShapeDtypeStruct((rows + gain.shape[1] // HEAD_WIDTH, 2 * HEAD_WIDTH), BF16)
    return pl.pallas_call(
        functools.partial(attention_grad_kernel, n_f, n_c),
        out_shape=(jax.ShapeDtypeStruct((rows, width), BF16),) + (dkv,) * n_c,
        in_specs=[SMEM] + [VMEM] * (7 + n_c),
        out_specs=(VMEM,) * (1 + n_c),
        compiler_params=params(24),
        cost_estimate=cost(4),
        name="attention_gradients",
    )(f, *pieces, queries, att, lse, gain, grad_a, grad_b, w_out)


def norm_kernel(resid_ref, gain_ref, *refs):
    terms, (hidden_ref, normed_ref) = refs[:-2], refs[-2:]
    total = resid_ref[...].astype(F32)
    total = total + functools.reduce(jnp.add, [t[...].astype(F32) for t in terms])
    hidden = total.astype(BF16)
    hidden_ref[...] = hidden
    hidden = hidden.astype(F32)
    inv_rms = lax.rsqrt(jnp.mean(hidden * hidden, axis=1, keepdims=True) + norm_eps)
    normed_ref[...] = (hidden * inv_rms * gain_ref[...]).astype(BF16)


def norm_call(resid, gain_row, terms):
    out = jax.ShapeDtypeStruct(resid.shape, BF16)
    return pl.pallas_call(
        norm_kernel,
        out_shape=(out, out),
        in_specs=[VMEM] * (2 + len(terms)),
        out_specs=[VMEM] * 2,
        compiler_params=params(8),
        cost_estimate=cost(8),
        name="residual_and_norm",
    )(resid, gain_row, *terms)


def norm_grad_kernel(cot_ref, hidden_ref, gain_ref, *refs):
    terms, (grad_ref, copy_ref, gain_grad_ref) = refs[:-3], refs[-3:]
    grad_normed = functools.reduce(jnp.add, [t[...].astype(F32) for t in terms])
    hidden = hidden_ref[...].astype(F32)
    inv_rms = lax.rsqrt(jnp.mean(hidden * hidden, axis=1, keepdims=True) + norm_eps)
    gained = grad_normed * gain_ref[...]
    inv_cube = inv_rms * inv_rms * inv_rms
    grad = (
        cot_ref[...].astype(F32)
        + inv_rms * gained
        - hidden * inv_cube * jnp.mean(gained * hidden, axis=1, keepdims=True)
    ).astype(BF16)
    grad_ref[...] = grad
    copy_ref[...] = grad
    gain_grad_ref[...] = jnp.sum(grad_normed * hidden * inv_rms, axis=0, keepdims=True)


def norm_grad_call(cot, hidden, gain_row, terms):
    return pl.pallas_call(
        norm_grad_kernel,
        out_shape=(
            jax.ShapeDtypeStruct(cot.shape, BF16),
            jax.ShapeDtypeStruct(cot.shape, BF16),
            jax.ShapeDtypeStruct(gain_row.shape, F32),
        ),
        in_specs=[VMEM] * (3 + len(terms)),
        out_specs=[VMEM] * 3,
        compiler_params=params(8),
        cost_estimate=cost(8),
        name="norm_gradients",
    )(cot, hidden, gain_row, *terms)


def gate_up_kernel(xa_ref, xb_ref, wg_ref, wu_ref, ga_ref, out_ref, gate_acc, up_acc):
    depth, width = wg_ref.shape
    half = xa_ref.shape[0]
    tile = 512
    gate_acc[...] = jnp.zeros_like(gate_acc)
    up_acc[...] = jnp.zeros_like(up_acc)

    @pl.loop(0, depth // tile)
    def _(step):
        at = pl.ds(pl.multiple_of(step * tile, tile), tile)
        x = jnp.concatenate([xa_ref[:, at], xb_ref[:, at]], axis=0)
        gate_acc[...] += dot(x, wg_ref[at, :])
        up_acc[...] += dot(x, wu_ref[at, :])

    gate, up, grad_act = gate_acc[...], up_acc[...], ga_ref[...]
    sig = jax.nn.sigmoid(gate)
    out_ref[:, :width] = (gate * sig * up).astype(BF16)
    out_ref[:, width : 2 * width] = (grad_act * up * sig * (1.0 + gate * (1.0 - sig))).astype(BF16)
    out_ref[:, 2 * width :] = (grad_act * gate * sig).astype(BF16)


def gate_up_call(xa, xb, w_gate, w_up, grad_act):
    depth, width = w_gate.shape
    rows = grad_act.shape[0]
    return pl.pallas_call(
        gate_up_kernel,
        out_shape=jax.ShapeDtypeStruct((rows, 3 * width), BF16),
        in_specs=[VMEM] * 5,
        out_specs=VMEM,
        scratch_shapes=[pltpu.VMEM((rows, width), F32)] * 2,
        compiler_params=params(24),
        cost_estimate=cost(2),
        name="gate_up_and_gradients",
    )(xa, xb, w_gate, w_up, grad_act)


def normed_grad_kernel(pay_ref, wg_ref, wu_ref, keep_ref, give_ref):
    depth, width = wg_ref.shape
    half = keep_ref.shape[0]
    tile = 512

    @pl.loop(0, depth // tile)
    def _(step):
        at = pl.ds(pl.multiple_of(step * tile, tile), tile)
        out = dot(pay_ref[:, width : 2 * width], wg_ref[at, :], NT)
        out = (out + dot(pay_ref[:, 2 * width :], wu_ref[at, :], NT)).astype(BF16)
        keep_ref[:, at] = out[:half]
        give_ref[:, at] = out[half:]


def normed_grad_call(pay, w_gate, w_up):
    depth, width = w_gate.shape
    rows = pay.shape[0]
    out = jax.ShapeDtypeStruct((rows // 2, depth), BF16)
    return pl.pallas_call(
        normed_grad_kernel,
        out_shape=(out, out),
        in_specs=[VMEM] * 3,
        out_specs=[VMEM] * 2,
        compiler_params=params(24),
        cost_estimate=cost(2),
        name="normed_gradients",
    )(pay, w_gate, w_up)


def column_blocks_kernel(c_ref, a_ref, *out_refs):
    cols = a_ref.shape[1] // len(out_refs)
    for k, out_ref in enumerate(out_refs):
        start = pl.multiple_of((c_ref[0] ^ k) * cols, 128)
        out_ref[...] = a_ref[:, pl.ds(start, cols)]


def column_blocks(c, a, n_c):
    rows, depth = a.shape
    return pl.pallas_call(
        column_blocks_kernel,
        out_shape=(jax.ShapeDtypeStruct((rows, depth // n_c), BF16),) * n_c,
        in_specs=[SMEM, VMEM],
        out_specs=(VMEM,) * n_c,
        compiler_params=params(8),
        cost_estimate=cost(1),
        name="column_blocks",
    )(c, a)


def take(refs, pieces, width):
    return jnp.concatenate([refs[i][r : r + n, at : at + width] for i, r, n, at in pieces], axis=0)


def weight_grad_kernel(left, right, n_left, tiled, *refs):
    operands, (out_hbm, out_ref, sems) = refs[:-3], refs[-3:]
    height, width = out_ref.shape
    left_refs, right_refs = operands[:n_left], operands[n_left:]
    tile = 256
    copies = []
    fixed = take(right_refs, right, width) if tiled == 0 else take(left_refs, left, height)
    for n, at in enumerate(range(0, out_ref.shape[tiled], tile)):
        size = min(tile, out_ref.shape[tiled] - at)
        if tiled == 0:
            moving = take(left_refs, [(i, r, m, first + at) for i, r, m, first in left], size)
            where = (pl.ds(at, size), slice(None))
            out_ref[where] = dot(moving, fixed, TN)
        else:
            moving = take(right_refs, [(i, r, m, first + at) for i, r, m, first in right], size)
            where = (slice(None), pl.ds(at, size))
            out_ref[where] = dot(fixed, moving, TN)
        copies.append(pltpu.make_async_copy(out_ref.at[where], out_hbm.at[where], sems.at[n]))
        copies[-1].start()
    for copy in copies:
        copy.wait()


def weight_grad_call(left, left_refs, right, right_refs, widths, tiled, name):
    return pl.pallas_call(
        functools.partial(weight_grad_kernel, left, right, len(left_refs), tiled),
        out_shape=jax.ShapeDtypeStruct(widths, F32),
        in_specs=[VMEM] * (len(left_refs) + len(right_refs)),
        out_specs=ANY,
        scratch_shapes=[
            pltpu.VMEM(widths, F32),
            pltpu.SemaphoreType.DMA((-(-widths[tiled] // 256),)),
        ],
        compiler_params=params(20),
        cost_estimate=cost(3),
        name=name,
    )(*left_refs, *right_refs)


def tree_sum(values):
    while len(values) > 1:
        values = [values[i] + values[i + 1] for i in range(0, len(values), 2)]
    return values[0]


def sum_kernel(n_f, rows, f_ref, *refs):
    parts, (own_ref, beside_ref, total_ref) = refs[:-3], refs[-3:]
    share, lines = rows // n_f, (parts[0].shape[0] - rows) // 2
    total_ref[...] = tree_sum([p[:rows, :].astype(F32) for p in parts])
    gain = tree_sum(
        [p[rows : rows + lines, :].astype(F32) + p[rows + lines :, :].astype(F32) for p in parts]
    )
    high = gain.astype(BF16)
    low = (gain - high.astype(F32)).astype(BF16)
    for k in range(n_f):
        out_ref = (own_ref, beside_ref)[k % 2]
        start = pl.multiple_of((f_ref[0] ^ k) * share, share)
        out_ref[k // 2, :lines, :] = high
        out_ref[k // 2, lines : 2 * lines, :] = low
        out_ref[k // 2, 2 * lines :, :] = total_ref[pl.ds(start, share), :].astype(BF16)


def sum_call(f, parts, rows, n_f):
    lines = parts[0].shape[0] - rows
    out = jax.ShapeDtypeStruct((n_f // 2, lines + rows // n_f, 2 * HEAD_WIDTH), BF16)
    return pl.pallas_call(
        functools.partial(sum_kernel, n_f, rows),
        out_shape=(out, out),
        in_specs=[SMEM] + [VMEM] * len(parts),
        out_specs=(VMEM, VMEM),
        scratch_shapes=[pltpu.VMEM((rows, 2 * HEAD_WIDTH), F32)],
        compiler_params=params(8),
        cost_estimate=cost(1),
        name="sum_over_ctx",
    )(f, *parts)


def heads_kernel(n_f, f_ref, *refs):
    in_refs, (dk_ref, dv_ref, gain_ref) = refs[:-3], refs[-3:]
    per_head = n_f // KEY_VALUE_HEADS
    width = 2 * HEAD_WIDTH
    lines = gain_ref.shape[1] // width
    chunks = [(ref, i) for ref in in_refs for i in range(2)]
    for k in range(0, n_f, per_head):
        total = tree_sum([r[i, 2 * lines :, :].astype(F32) for r, i in chunks[k : k + per_head]])
        head = lax.shift_right_logical(f_ref[0] ^ k, log2(per_head))
        at = pl.ds(pl.multiple_of(head * HEAD_WIDTH, HEAD_WIDTH), HEAD_WIDTH)
        dk_ref[:, at] = total[:, :HEAD_WIDTH]
        dv_ref[:, at] = total[:, HEAD_WIDTH:]
    gain = tree_sum(
        [
            r[i, :lines, :].astype(F32) + r[i, lines : 2 * lines, :].astype(F32)
            for r, i in chunks
        ]
    )
    for i in range(lines):
        gain_ref[:, i * width : (i + 1) * width] = gain[i : i + 1]


def heads_call(f, pairs, depth, n_f):
    share = pairs[0].shape[1] - depth // HEAD_WIDTH
    out = jax.ShapeDtypeStruct((share, KEY_VALUE_HEADS * HEAD_WIDTH), F32)
    return pl.pallas_call(
        functools.partial(heads_kernel, n_f),
        out_shape=(out, out, jax.ShapeDtypeStruct((1, depth), F32)),
        in_specs=[SMEM] + [VMEM] * len(pairs),
        out_specs=[VMEM] * 3,
        compiler_params=params(8),
        cost_estimate=cost(1),
        name="place_heads",
    )(f, *pairs)


def body(
    resid_in,
    queries,
    keys_in,
    value_rows_input,
    w_out,
    norm_gain,
    w_gate,
    w_up,
    w_down,
    cotangent,
    positions,
    doc_ids,
):
    rows = queries.shape[0]
    heads = queries.shape[1] // HEAD_WIDTH
    n_c, n_f = lax.axis_size("ctx"), lax.axis_size("ffn")
    c, f = lax.axis_index("ctx"), lax.axis_index("ffn")
    share, half = rows // n_f, n_f // 2
    depth = resid_in.shape[1]
    hidden_units = w_gate.shape[1]
    group = f * heads // (QUERY_HEADS // KEY_VALUE_HEADS)
    gain_row = norm_gain.reshape(1, depth)

    def exchange(x, axis, k):
        return lax.ppermute(x, axis, [(i, i ^ k) for i in range(lax.axis_size(axis))])

    def gather_rows(x):
        return jnp.concatenate([x] + [exchange(x, "ffn", 2 * m) for m in range(1, half)], axis=0)

    def beside(x):
        return exchange(x, "ffn", 1)

    def pair_sum(keep, give):
        return (keep.astype(F32) + beside(give).astype(F32)).astype(BF16)

    def scatter_rows(total):
        blocks = [total[m * share : (m + 1) * share] for m in range(half)]
        return [blocks[0]] + [exchange(blocks[m], "ffn", 2 * m) for m in range(1, half)]

    def after(x, *earlier):
        return lax.optimization_barrier((x, earlier))[0]

    bits = range(log2(n_c))

    def to_columns(blocks):
        return [blocks[0]] + [exchange(blocks[k], "ctx", k) for k in range(1, n_c)]

    cols = depth // n_c
    width = heads * HEAD_WIDTH
    pair = rows // 2
    f_ref = f.astype(jnp.int32).reshape(1)
    c_ref = c.astype(jnp.int32).reshape(1)
    q_rel, payload = prepare_call(
        f_ref,
        group.astype(jnp.int32).reshape(1),
        queries,
        keys_in,
        value_rows_input,
        positions.reshape(1, -1),
        doc_ids.reshape(1, -1),
        n_f,
    )
    pieces = [payload] + [exchange(payload, "ctx", k) for k in range(1, n_c)]
    cot_a = gather_rows(cotangent)

    keep, give, att, lse = attention_call(f_ref, q_rel, w_out, pieces, n_f)
    total = after(pair_sum(keep, give), cot_a)
    terms = scatter_rows(total)
    cot_b = beside(after(cot_a, total))
    terms[0] = after(terms[0], cot_b)
    hidden, normed = norm_call(resid_in, gain_row, terms)

    assert 2 * width == cols
    cot_late = after(cot_a, normed)
    cot_blocks = list(column_blocks(c_ref, cot_late, n_c))
    att_blocks = [jnp.concatenate([att[:pair], att[pair:]], axis=1)]

    def crossing(bit):
        moving = [k for k in range(n_c) if k >> bit & 1]
        return moving, jnp.concatenate([cot_blocks[k] for k in moving] + att_blocks, axis=0)

    def crossed(moving, message):
        parts = [message[i : i + pair] for i in range(0, message.shape[0], pair)]
        for k, part in zip(moving, parts):
            cot_blocks[k] = part
        att_blocks.extend(parts[len(moving) :])

    normed_a = gather_rows(normed)
    for bit in bits:
        moving, message = crossing(bit)
        if bit == bits[-1]:
            grad_act = dot(jnp.concatenate([cot_a, cot_b], axis=0), w_down, NT)
            normed_a = after(normed_a, grad_act, message)
        crossed(moving, exchange(message, "ctx", 1 << bit))
    normed_b = beside(normed_a)

    pay = gate_up_call(normed_a, normed_b, w_gate, w_up, grad_act)
    keep, give = normed_grad_call(pay, w_gate, w_up)
    total = pair_sum(keep, give)
    terms = scatter_rows(total)

    cot_cols = after(jnp.concatenate(cot_blocks, axis=0), total)
    cot_side = beside(cot_cols)

    late, normed_late = after((pay, normed_a), total)
    normed_blocks = column_blocks(c_ref, normed_late, n_c)

    class Half:
        def __init__(self, side):
            self.side = side
            self.order = list(bits) if side == 0 else list(bits)[::-1]
            lanes = slice(side * cols // 2, (side + 1) * cols // 2)
            self.columns = [block[:, lanes] for block in normed_blocks]
            self.arrays = [late]
            self.rows = {0: (0, side * pair, 0)}

        def row(self, k):
            array, start, at = self.rows[k]
            return self.arrays[array][start : start + pair, at : at + 3 * hidden_units]

        def message(self, step):
            bit = self.order[step]
            self.held = list(self.rows)
            self.moving = [k for k in range(n_c) if k >> bit & 1]
            parts = [self.row(k) for k in self.held] + [self.columns[k] for k in self.moving]
            return jnp.concatenate(parts, axis=1)

        def send(self, step, message):
            bit = self.order[step]
            self.arrays.append(exchange(message, "ctx", 1 << bit))
            at = 0
            for k in self.held:
                self.rows[k | 1 << bit] = (len(self.arrays) - 1, 0, at)
                at += 3 * hidden_units
            for k in self.moving:
                self.columns[k] = self.arrays[-1][:, at : at + cols // 2]
                at += cols // 2

    halves = [Half(0), Half(1)]
    for step in bits:
        messages = [h.message(step) for h in halves]
        if step == bits[-1]:
            down = dot(late[:, :hidden_units], w_down).astype(BF16)
            terms[0] = after(terms[0], messages[0], messages[1], down)
            grad_resid, grad_send, gain_part = norm_grad_call(cotangent, hidden, gain_row, terms)
        for h, message in zip(halves, messages):
            h.send(step, message)

    grad_a = gather_rows(grad_send)
    down_total = pair_sum(down[:pair], down[pair:])
    grad_a = after(grad_a, down_total)
    grad_b = beside(grad_a)
    mixed_terms = scatter_rows(after(down_total, grad_a))

    grad_queries, *parts = attention_grad_call(
        f_ref, q_rel, att, lse, gain_part, grad_a, grad_b, w_out, pieces, n_f
    )
    parts = [parts[0]] + [exchange(parts[k], "ctx", k) for k in range(1, n_c)]
    grad_cols = to_columns(column_blocks(c_ref, after(grad_a, *parts), n_c))
    grad_cols = jnp.concatenate(grad_cols, axis=0)
    grad_side = beside(grad_cols)

    own_chunks, beside_chunks = sum_call(f_ref, parts, rows, n_f)
    chunks = jnp.stack([own_chunks, beside(beside_chunks)], axis=1)
    chunks = [chunks[0]] + [exchange(chunks[m], "ffn", 2 * m) for m in range(1, half)]
    grad_keys, grad_values, grad_gain = heads_call(f_ref, chunks, depth, n_f)

    normed_cols = jnp.concatenate(
        [jnp.concatenate([h.columns[k] for h in halves], axis=1) for k in range(n_c)], axis=0
    )
    normed_cols = after(normed_cols, parts[0])
    normed_side = beside(normed_cols)
    offset = len(halves[0].arrays)
    hidden_refs = halves[0].arrays + halves[1].arrays

    def hidden_part(i):
        pieces = []
        for side, h in enumerate(halves):
            for k in range(n_c):
                array, start, at = h.rows[k]
                pieces.append((array + side * offset, start, pair, at + i * hidden_units))
        return pieces

    columns = [(0, 0, n_c * pair, 0), (1, 0, n_c * pair, 0)]
    att_rows = [(k, 0, pair, 0) for k in range(n_c)] + [(k, 0, pair, width) for k in range(n_c)]
    normed_pair, shape = (normed_cols, normed_side), (cols, hidden_units)
    grad_w_gate = weight_grad_call(
        columns, normed_pair, hidden_part(1), hidden_refs, shape, 0, "grad_w_gate"
    )
    grad_w_up = weight_grad_call(
        columns, normed_pair, hidden_part(2), hidden_refs, shape, 0, "grad_w_up"
    )
    grad_w_down = weight_grad_call(
        hidden_part(0), hidden_refs, columns, (cot_cols, cot_side), shape[::-1], 1, "grad_w_down"
    )
    grad_w_out = weight_grad_call(
        att_rows, att_blocks, columns, (grad_cols, grad_side), (width, cols), 1, "grad_w_out"
    )

    mixed = functools.reduce(jnp.add, [t.astype(F32) for t in mixed_terms])
    mixed = (hidden.astype(F32) + mixed).astype(BF16)

    return (
        mixed,
        grad_resid,
        grad_queries,
        grad_keys,
        grad_values,
        grad_gain.reshape(depth),
        grad_w_out,
        grad_w_gate,
        grad_w_up,
        grad_w_down,
    )


def solution(mesh):
    return jax.shard_map(
        body,
        mesh=mesh,
        in_specs=(
            P(("ctx", "ffn"), None),
            P("ctx", "ffn"),
            P("ctx", None),
            P("ctx", None),
            P("ffn", None),
            P(),
            P(None, "ffn"),
            P(None, "ffn"),
            P("ffn", None),
            P(("ctx", "ffn"), None),
            P("ctx"),
            P(),
        ),
        out_specs=(
            P(("ctx", "ffn"), None),
            P(("ctx", "ffn"), None),
            P("ctx", "ffn"),
            P(("ctx", "ffn"), None),
            P(("ctx", "ffn"), None),
            P(),
            P("ffn", "ctx"),
            P("ctx", "ffn"),
            P("ctx", "ffn"),
            P("ffn", "ctx"),
        ),
        check_vma=False,
    )
```

```python
import functools
import math

import jax
import jax.numpy as jnp
from jax import lax
from jax.experimental import pallas as pl
from jax.experimental.pallas import tpu as pltpu
from jax.sharding import PartitionSpec as P

QUERY_HEADS = 32
KEY_VALUE_HEADS = 8
HEAD_WIDTH = 128
STRIPE = 64

masked_fill = -1e30
norm_eps = 1e-05
score_scale = 1.0 / math.sqrt(HEAD_WIDTH)

F32 = jnp.float32
BF16 = jnp.bfloat16
NN = (((1,), (0,)), ((), ()))
NT = (((1,), (1,)), ((), ()))
TN = (((0,), (0,)), ((), ()))
VMEM = pl.BlockSpec(memory_space=pltpu.VMEM)
SMEM = pl.BlockSpec(memory_space=pltpu.SMEM)
ANY = pl.BlockSpec(memory_space=pl.ANY)


def dot(a, b, dims=NN):
    return lax.dot_general(a, b, dims, preferred_element_type=F32)


def params(megabytes=48):
    return pltpu.CompilerParams(vmem_limit_bytes=megabytes * 1024 * 1024)


def cost(microseconds):
    return pl.CostEstimate(
        flops=int(microseconds * 5e8), bytes_accessed=int(microseconds * 2e6), transcendentals=0
    )


def fetch(sources, targets, sems):
    copies = [pltpu.make_async_copy(s, t, sems.at[i]) for i, (s, t) in enumerate(zip(sources, targets))]
    for copy in copies:
        copy.start()
    return copies


def scratch_like(*arrays):
    return [pltpu.VMEM(a.shape, a.dtype) for a in arrays] + [
        pltpu.SemaphoreType.DMA((len(arrays),))
    ]


def log2(n):
    assert n & (n - 1) == 0
    return n.bit_length() - 1


def relative_rows(f, rows, n_f):
    share, half = rows // n_f, n_f // 2
    r = lax.broadcasted_iota(jnp.int32, (rows, rows), 0)
    natural = lax.broadcasted_iota(jnp.int32, (rows, rows), 1)
    j = lax.shift_right_logical(r, log2(share))
    k = lax.shift_left(j & (half - 1), 1) | lax.shift_right_logical(j, log2(half))
    return natural == lax.shift_left(k ^ f, log2(share)) + (r & (share - 1))


def visibility(same_row, pieces, rows):
    coded = [piece[2 * rows :, :].astype(F32) for piece in pieces]
    key_pos = jnp.concatenate([t[0:1] * STRIPE + t[1:2] for t in coded], axis=1)
    key_seg = jnp.concatenate([t[2:3] for t in coded], axis=1)

    def to_column(row):
        return jnp.sum(jnp.where(same_row, row[:, :rows], 0.0), axis=1, keepdims=True)

    return (key_pos <= to_column(key_pos)) & (key_seg == to_column(key_seg))


def keys_and_values(pieces, rows):
    return (
        jnp.concatenate([p[:rows] for p in pieces], axis=0),
        jnp.concatenate([p[rows : 2 * rows] for p in pieces], axis=0),
    )


def prepare_kernel(
    n_f, f_ref, group_ref, q_hbm, k_hbm, v_hbm, pos_hbm, doc_hbm, q_out, payload, *scratch
):
    q_ref, pos_ref, doc_ref, sems = scratch
    rows = q_ref.shape[0]
    cols = pl.ds(pl.multiple_of(group_ref[0] * HEAD_WIDTH, HEAD_WIDTH), HEAD_WIDTH)
    copies = fetch(
        [pos_hbm, doc_hbm, q_hbm, k_hbm.at[:, cols], v_hbm.at[:, cols]],
        [pos_ref, doc_ref, q_ref, payload.at[pl.ds(0, rows)], payload.at[pl.ds(rows, rows)]],
        sems,
    )
    same_row = relative_rows(f_ref[0], rows, n_f)
    line = lax.broadcasted_iota(jnp.int32, (16, rows), 0)
    copies[0].wait()
    copies[1].wait()
    pos = pos_ref[...]
    total = doc_ref.shape[1]
    where_is = lax.broadcasted_iota(jnp.int32, (total, rows), 0) == pos
    docs = jnp.broadcast_to(doc_ref[...].astype(F32), (8, total)).astype(BF16)
    seg = dot(docs, where_is.astype(F32).astype(BF16))[0:1]
    high = lax.shift_right_logical(pos, log2(STRIPE))
    low = pos & (STRIPE - 1)
    coded = jnp.where(line == 0, high.astype(F32), jnp.where(line == 1, low.astype(F32), 0.0))
    payload[2 * rows :, :] = jnp.where(line == 2, seg, coded).astype(BF16)
    copies[2].wait()
    q_out[...] = dot(same_row.astype(F32).astype(BF16), q_ref[...]).astype(BF16)
    copies[3].wait()
    copies[4].wait()


def prepare_call(f, group, queries, keys_in, values_in, pos_row, doc_row, n_f):
    rows = queries.shape[0]
    assert rows == HEAD_WIDTH
    return pl.pallas_call(
        functools.partial(prepare_kernel, n_f),
        out_shape=(
            jax.ShapeDtypeStruct(queries.shape, BF16),
            jax.ShapeDtypeStruct((2 * rows + 16, HEAD_WIDTH), BF16),
        ),
        in_specs=[SMEM, SMEM] + [ANY] * 5,
        out_specs=[VMEM] * 2,
        scratch_shapes=scratch_like(queries, pos_row, doc_row)[:-1]
        + [pltpu.SemaphoreType.DMA((5,))],
        compiler_params=params(58),
        cost_estimate=cost(2),
        name="prepare_attention",
    )(f, group, queries, keys_in, values_in, pos_row, doc_row)


def attention_kernel(n_f, n_c, f_ref, *refs):
    sources, refs = refs[: n_c + 2], refs[n_c + 2 :]
    (keep_ref, give_ref, att_ref, lse_ref), scratch, sems = refs[:4], refs[4:-1], refs[-1]
    copies = fetch(sources, scratch, sems)
    q_ref, pieces, w_ref = scratch[0], scratch[1:-1], scratch[-1]
    for copy in copies[:-1]:
        copy.wait()
    rows, width = q_ref.shape
    same_row = relative_rows(f_ref[0], rows, n_f)
    visible = visibility(same_row, pieces, rows)
    keys, values = keys_and_values(pieces, rows)
    q = q_ref[...]
    lane = lax.broadcasted_iota(jnp.int32, (rows, HEAD_WIDTH), 1)
    log_totals = jnp.zeros((rows, HEAD_WIDTH), F32)
    for h in range(width // HEAD_WIDTH):
        cols = slice(h * HEAD_WIDTH, (h + 1) * HEAD_WIDTH)
        scores = jnp.where(visible, dot(q[:, cols], keys, NT) * score_scale, masked_fill)
        row_max = jnp.max(scores, axis=1, keepdims=True)
        weights = jnp.exp(scores - row_max)
        row_total = jnp.sum(weights, axis=1, keepdims=True)
        att_ref[:, cols] = (dot(weights.astype(BF16), values) / row_total).astype(BF16)
        log_totals = jnp.where(lane == h, row_max + jnp.log(row_total), log_totals)
    lse_ref[...] = log_totals
    copies[-1].wait()
    att = att_ref[...]
    tile = 512
    for start in range(0, w_ref.shape[1], tile):
        out = dot(att, w_ref[:, start : start + tile]).astype(BF16)
        keep_ref[:, start : start + tile] = out[: rows // 2]
        give_ref[:, start : start + tile] = out[rows // 2 :]


def attention_call(f, queries, w_out, pieces, n_f):
    rows, width = queries.shape
    depth = w_out.shape[1]
    half = jax.ShapeDtypeStruct((rows // 2, depth), BF16)
    att = jax.ShapeDtypeStruct((rows, width), BF16)
    lse = jax.ShapeDtypeStruct((rows, HEAD_WIDTH), F32)
    return pl.pallas_call(
        functools.partial(attention_kernel, n_f, len(pieces)),
        out_shape=(half, half, att, lse),
        in_specs=[SMEM] + [ANY] * (2 + len(pieces)),
        out_specs=[VMEM] * 4,
        scratch_shapes=scratch_like(queries, *pieces, w_out),
        compiler_params=params(56),
        cost_estimate=cost(4),
        name="attention_and_projection",
    )(f, queries, *pieces, w_out)


def fold(row):
    width = 2 * HEAD_WIDTH
    return [row[:, i : i + width] for i in range(0, row.shape[1], width)]


def attention_grad_kernel(n_f, n_c, f_ref, *refs):
    pieces, refs = refs[:n_c], refs[n_c:]
    q_ref, att_ref, lse_ref, gain_ref, ga_ref, gb_ref, w_ref = refs[:7]
    dq_ref, dkv_refs = refs[7], refs[8:]
    rows, width = q_ref.shape
    same_row = relative_rows(f_ref[0], rows, n_f)
    visible = visibility(same_row, pieces, rows)
    keys, values = keys_and_values(pieces, rows)
    order = same_row.astype(F32).astype(BF16)
    q = q_ref[...]
    grad_rows = jnp.concatenate([ga_ref[...], gb_ref[...]], axis=0)
    grad_att = dot(grad_rows, w_ref[...], NT).astype(BF16)
    grad_keys = jnp.zeros(keys.shape, F32)
    grad_values = jnp.zeros(keys.shape, F32)
    grad_q = []
    for h in range(width // HEAD_WIDTH):
        cols = slice(h * HEAD_WIDTH, (h + 1) * HEAD_WIDTH)
        g = grad_att[:, cols]
        scores = jnp.where(visible, dot(q[:, cols], keys, NT) * score_scale, masked_fill)
        probs = jnp.exp(scores - lse_ref[:, h : h + 1])
        delta = jnp.sum(g.astype(F32) * att_ref[:, cols].astype(F32), axis=1, keepdims=True)
        grad_scores = (probs * (dot(g, values, NT) - delta)).astype(BF16)
        grad_q.append((dot(grad_scores, keys) * score_scale).astype(BF16))
        grad_keys = grad_keys + dot(grad_scores, q[:, cols], TN)
        grad_values = grad_values + dot(probs.astype(BF16), g, TN)
    dq_ref[...] = dot(order, jnp.concatenate(grad_q, axis=1), TN).astype(BF16)
    high = gain_ref[...].astype(BF16)
    low = (gain_ref[...] - high.astype(F32)).astype(BF16)
    lines = fold(high) + fold(low)
    for k, dkv_ref in enumerate(dkv_refs):
        part = slice(k * rows, (k + 1) * rows)
        dkv_ref[:rows, :HEAD_WIDTH] = (grad_keys[part] * score_scale).astype(BF16)
        dkv_ref[:rows, HEAD_WIDTH:] = grad_values[part].astype(BF16)
        for i, line in enumerate(lines):
            dkv_ref[rows + i : rows + i + 1, :] = line


def attention_grad_call(f, queries, att, lse, gain, grad_a, grad_b, w_out, pieces, n_f):
    rows, width = queries.shape
    n_c = len(pieces)
    dkv = jax.ShapeDtypeStruct((rows + gain.shape[1] // HEAD_WIDTH, 2 * HEAD_WIDTH), BF16)
    return pl.pallas_call(
        functools.partial(attention_grad_kernel, n_f, n_c),
        out_shape=(jax.ShapeDtypeStruct((rows, width), BF16),) + (dkv,) * n_c,
        in_specs=[SMEM] + [VMEM] * (7 + n_c),
        out_specs=(VMEM,) * (1 + n_c),
        compiler_params=params(24),
        cost_estimate=cost(4),
        name="attention_gradients",
    )(f, *pieces, queries, att, lse, gain, grad_a, grad_b, w_out)


def norm_kernel(resid_ref, gain_ref, *refs):
    terms, (hidden_ref, normed_ref) = refs[:-2], refs[-2:]
    total = resid_ref[...].astype(F32)
    total = total + functools.reduce(jnp.add, [t[...].astype(F32) for t in terms])
    hidden = total.astype(BF16)
    hidden_ref[...] = hidden
    hidden = hidden.astype(F32)
    inv_rms = lax.rsqrt(jnp.mean(hidden * hidden, axis=1, keepdims=True) + norm_eps)
    normed_ref[...] = (hidden * inv_rms * gain_ref[...]).astype(BF16)


def norm_call(resid, gain_row, terms):
    out = jax.ShapeDtypeStruct(resid.shape, BF16)
    return pl.pallas_call(
        norm_kernel,
        out_shape=(out, out),
        in_specs=[VMEM] * (2 + len(terms)),
        out_specs=[VMEM] * 2,
        compiler_params=params(8),
        cost_estimate=cost(8),
        name="residual_and_norm",
    )(resid, gain_row, *terms)


def norm_grad_kernel(cot_ref, hidden_ref, gain_ref, *refs):
    terms, (grad_ref, copy_ref, gain_grad_ref) = refs[:-3], refs[-3:]
    grad_normed = functools.reduce(jnp.add, [t[...].astype(F32) for t in terms])
    hidden = hidden_ref[...].astype(F32)
    inv_rms = lax.rsqrt(jnp.mean(hidden * hidden, axis=1, keepdims=True) + norm_eps)
    gained = grad_normed * gain_ref[...]
    inv_cube = inv_rms * inv_rms * inv_rms
    grad = (
        cot_ref[...].astype(F32)
        + inv_rms * gained
        - hidden * inv_cube * jnp.mean(gained * hidden, axis=1, keepdims=True)
    ).astype(BF16)
    grad_ref[...] = grad
    copy_ref[...] = grad
    gain_grad_ref[...] = jnp.sum(grad_normed * hidden * inv_rms, axis=0, keepdims=True)


def norm_grad_call(cot, hidden, gain_row, terms):
    return pl.pallas_call(
        norm_grad_kernel,
        out_shape=(
            jax.ShapeDtypeStruct(cot.shape, BF16),
            jax.ShapeDtypeStruct(cot.shape, BF16),
            jax.ShapeDtypeStruct(gain_row.shape, F32),
        ),
        in_specs=[VMEM] * (3 + len(terms)),
        out_specs=[VMEM] * 3,
        compiler_params=params(8),
        cost_estimate=cost(8),
        name="norm_gradients",
    )(cot, hidden, gain_row, *terms)


def gate_up_kernel(xa_ref, xb_ref, wg_ref, wu_ref, ga_ref, out_ref):
    width = wg_ref.shape[1]
    x = jnp.concatenate([xa_ref[...], xb_ref[...]], axis=0)
    tile = 256
    for start in range(0, width, tile):
        end = min(start + tile, width)
        gate, up = dot(x, wg_ref[:, start:end]), dot(x, wu_ref[:, start:end])
        grad_act = ga_ref[:, start:end]
        sig = jax.nn.sigmoid(gate)
        out_ref[:, start:end] = (gate * sig * up).astype(BF16)
        grad_gate = grad_act * up * sig * (1.0 + gate * (1.0 - sig))
        out_ref[:, width + start : width + end] = grad_gate.astype(BF16)
        out_ref[:, 2 * width + start : 2 * width + end] = (grad_act * gate * sig).astype(BF16)


def gate_up_call(xa, xb, w_gate, w_up, grad_act):
    depth, width = w_gate.shape
    rows = grad_act.shape[0]
    return pl.pallas_call(
        gate_up_kernel,
        out_shape=jax.ShapeDtypeStruct((rows, 3 * width), BF16),
        in_specs=[VMEM] * 5,
        out_specs=VMEM,
        compiler_params=params(24),
        cost_estimate=cost(2),
        name="gate_up_and_gradients",
    )(xa, xb, w_gate, w_up, grad_act)


def normed_grad_kernel(pay_ref, wg_ref, wu_ref, keep_ref, give_ref):
    depth, width = wg_ref.shape
    half = keep_ref.shape[0]
    grad_gate, grad_up = pay_ref[:, width : 2 * width], pay_ref[:, 2 * width :]
    tile = 1024
    for start in range(0, depth, tile):
        at = slice(start, start + tile)
        out = dot(wg_ref[at, :], grad_gate, NT) + dot(wu_ref[at, :], grad_up, NT)
        out = out.T.astype(BF16)
        keep_ref[:, at] = out[:half]
        give_ref[:, at] = out[half:]


def normed_grad_call(pay, w_gate, w_up):
    depth, width = w_gate.shape
    rows = pay.shape[0]
    out = jax.ShapeDtypeStruct((rows // 2, depth), BF16)
    return pl.pallas_call(
        normed_grad_kernel,
        out_shape=(out, out),
        in_specs=[VMEM] * 3,
        out_specs=[VMEM] * 2,
        compiler_params=params(24),
        cost_estimate=cost(2),
        name="normed_gradients",
    )(pay, w_gate, w_up)


def column_blocks_kernel(c_ref, a_ref, *out_refs):
    cols = a_ref.shape[1] // len(out_refs)
    for k, out_ref in enumerate(out_refs):
        start = pl.multiple_of((c_ref[0] ^ k) * cols, 128)
        out_ref[...] = a_ref[:, pl.ds(start, cols)]


def column_blocks(c, a, n_c):
    rows, depth = a.shape
    return pl.pallas_call(
        column_blocks_kernel,
        out_shape=(jax.ShapeDtypeStruct((rows, depth // n_c), BF16),) * n_c,
        in_specs=[SMEM, VMEM],
        out_specs=(VMEM,) * n_c,
        compiler_params=params(8),
        cost_estimate=cost(1),
        name="column_blocks",
    )(c, a)


def take(refs, pieces, width):
    return jnp.concatenate([refs[i][r : r + n, at : at + width] for i, r, n, at in pieces], axis=0)


def weight_grad_kernel(left, right, n_left, tiled, *refs):
    operands, (out_hbm, out_ref, sems) = refs[:-3], refs[-3:]
    height, width = out_ref.shape
    left_refs, right_refs = operands[:n_left], operands[n_left:]
    tile = 256
    copies = []
    fixed = take(right_refs, right, width) if tiled == 0 else take(left_refs, left, height)
    for n, at in enumerate(range(0, out_ref.shape[tiled], tile)):
        size = min(tile, out_ref.shape[tiled] - at)
        if tiled == 0:
            moving = take(left_refs, [(i, r, m, first + at) for i, r, m, first in left], size)
            where = (pl.ds(at, size), slice(None))
            out_ref[where] = dot(moving, fixed, TN)
        else:
            moving = take(right_refs, [(i, r, m, first + at) for i, r, m, first in right], size)
            where = (slice(None), pl.ds(at, size))
            out_ref[where] = dot(fixed, moving, TN)
        copies.append(pltpu.make_async_copy(out_ref.at[where], out_hbm.at[where], sems.at[n]))
        copies[-1].start()
    for copy in copies:
        copy.wait()


def weight_grad_call(left, left_refs, right, right_refs, widths, tiled, name):
    return pl.pallas_call(
        functools.partial(weight_grad_kernel, left, right, len(left_refs), tiled),
        out_shape=jax.ShapeDtypeStruct(widths, F32),
        in_specs=[VMEM] * (len(left_refs) + len(right_refs)),
        out_specs=ANY,
        scratch_shapes=[
            pltpu.VMEM(widths, F32),
            pltpu.SemaphoreType.DMA((-(-widths[tiled] // 256),)),
        ],
        compiler_params=params(20),
        cost_estimate=cost(3),
        name=name,
    )(*left_refs, *right_refs)


def tree_sum(values):
    while len(values) > 1:
        values = [values[i] + values[i + 1] for i in range(0, len(values), 2)]
    return values[0]


def sum_kernel(n_f, rows, f_ref, *refs):
    parts, (own_ref, beside_ref, total_ref) = refs[:-3], refs[-3:]
    share, lines = rows // n_f, (parts[0].shape[0] - rows) // 2
    total_ref[...] = tree_sum([p[:rows, :].astype(F32) for p in parts])
    gain = tree_sum(
        [p[rows : rows + lines, :].astype(F32) + p[rows + lines :, :].astype(F32) for p in parts]
    )
    high = gain.astype(BF16)
    low = (gain - high.astype(F32)).astype(BF16)
    for k in range(n_f):
        out_ref = (own_ref, beside_ref)[k % 2]
        start = pl.multiple_of((f_ref[0] ^ k) * share, share)
        out_ref[k // 2, :lines, :] = high
        out_ref[k // 2, lines : 2 * lines, :] = low
        out_ref[k // 2, 2 * lines :, :] = total_ref[pl.ds(start, share), :].astype(BF16)


def sum_call(f, parts, rows, n_f):
    lines = parts[0].shape[0] - rows
    out = jax.ShapeDtypeStruct((n_f // 2, lines + rows // n_f, 2 * HEAD_WIDTH), BF16)
    return pl.pallas_call(
        functools.partial(sum_kernel, n_f, rows),
        out_shape=(out, out),
        in_specs=[SMEM] + [VMEM] * len(parts),
        out_specs=(VMEM, VMEM),
        scratch_shapes=[pltpu.VMEM((rows, 2 * HEAD_WIDTH), F32)],
        compiler_params=params(8),
        cost_estimate=cost(1),
        name="sum_over_ctx",
    )(f, *parts)


def heads_kernel(n_f, f_ref, *refs):
    in_refs, (dk_ref, dv_ref, gain_ref) = refs[:-3], refs[-3:]
    per_head = n_f // KEY_VALUE_HEADS
    width = 2 * HEAD_WIDTH
    lines = gain_ref.shape[1] // width
    chunks = [(ref, i) for ref in in_refs for i in range(2)]
    for k in range(0, n_f, per_head):
        total = tree_sum([r[i, 2 * lines :, :].astype(F32) for r, i in chunks[k : k + per_head]])
        head = lax.shift_right_logical(f_ref[0] ^ k, log2(per_head))
        at = pl.ds(pl.multiple_of(head * HEAD_WIDTH, HEAD_WIDTH), HEAD_WIDTH)
        dk_ref[:, at] = total[:, :HEAD_WIDTH]
        dv_ref[:, at] = total[:, HEAD_WIDTH:]
    gain = tree_sum(
        [
            r[i, :lines, :].astype(F32) + r[i, lines : 2 * lines, :].astype(F32)
            for r, i in chunks
        ]
    )
    for i in range(lines):
        gain_ref[:, i * width : (i + 1) * width] = gain[i : i + 1]


def heads_call(f, pairs, depth, n_f):
    share = pairs[0].shape[1] - depth // HEAD_WIDTH
    out = jax.ShapeDtypeStruct((share, KEY_VALUE_HEADS * HEAD_WIDTH), F32)
    return pl.pallas_call(
        functools.partial(heads_kernel, n_f),
        out_shape=(out, out, jax.ShapeDtypeStruct((1, depth), F32)),
        in_specs=[SMEM] + [VMEM] * len(pairs),
        out_specs=[VMEM] * 3,
        compiler_params=params(8),
        cost_estimate=cost(1),
        name="place_heads",
    )(f, *pairs)


def body(
    resid_in,
    queries,
    keys_in,
    value_rows_input,
    w_out,
    norm_gain,
    w_gate,
    w_up,
    w_down,
    cotangent,
    positions,
    doc_ids,
):
    rows = queries.shape[0]
    heads = queries.shape[1] // HEAD_WIDTH
    n_c, n_f = lax.axis_size("ctx"), lax.axis_size("ffn")
    c, f = lax.axis_index("ctx"), lax.axis_index("ffn")
    share, half = rows // n_f, n_f // 2
    depth = resid_in.shape[1]
    hidden_units = w_gate.shape[1]
    group = f * heads // (QUERY_HEADS // KEY_VALUE_HEADS)
    gain_row = norm_gain.reshape(1, depth)

    def exchange(x, axis, k):
        return lax.ppermute(x, axis, [(i, i ^ k) for i in range(lax.axis_size(axis))])

    def gather_rows(x):
        return jnp.concatenate([x] + [exchange(x, "ffn", 2 * m) for m in range(1, half)], axis=0)

    def beside(x):
        return exchange(x, "ffn", 1)

    def pair_sum(keep, give):
        return (keep.astype(F32) + beside(give).astype(F32)).astype(BF16)

    def scatter_rows(total):
        blocks = [total[m * share : (m + 1) * share] for m in range(half)]
        return [blocks[0]] + [exchange(blocks[m], "ffn", 2 * m) for m in range(1, half)]

    def after(x, *earlier):
        return lax.optimization_barrier((x, earlier))[0]

    bits = range(log2(n_c))

    def to_columns(blocks):
        return [blocks[0]] + [exchange(blocks[k], "ctx", k) for k in range(1, n_c)]

    cols = depth // n_c
    width = heads * HEAD_WIDTH
    pair = rows // 2
    f_ref = f.astype(jnp.int32).reshape(1)
    c_ref = c.astype(jnp.int32).reshape(1)
    q_rel, payload = prepare_call(
        f_ref,
        group.astype(jnp.int32).reshape(1),
        queries,
        keys_in,
        value_rows_input,
        positions.reshape(1, -1),
        doc_ids.reshape(1, -1),
        n_f,
    )
    pieces = [payload] + [exchange(payload, "ctx", k) for k in range(1, n_c)]
    cot_a = gather_rows(cotangent)

    keep, give, att, lse = attention_call(f_ref, q_rel, w_out, pieces, n_f)
    total = after(pair_sum(keep, give), cot_a)
    terms = scatter_rows(total)
    cot_b = beside(after(cot_a, total))
    terms[0] = after(terms[0], cot_b)

    assert 2 * width == cols
    cot_late = after(cot_a, cot_b)
    cot_blocks = list(column_blocks(c_ref, cot_late, n_c))
    att_blocks = [jnp.concatenate([att[:pair], att[pair:]], axis=1)]

    def split(message):
        return [message[i : i + pair] for i in range(0, message.shape[0], pair)]

    def owned(bit):
        return [k for k in range(n_c) if k >> bit & 1 and not k & ((1 << bit) - 1)]

    first_messages = [
        exchange(
            jnp.concatenate([cot_blocks[k] for k in owned(bit)] + att_blocks, axis=0),
            "ctx",
            1 << bit,
        )
        for bit in bits
    ]
    terms[0] = after(terms[0], first_messages)
    hidden, normed = norm_call(resid_in, gain_row, terms)
    normed_a = gather_rows(normed)
    for bit in bits:
        *blocks, att_block = split(first_messages[bit])
        for k, block in zip(owned(bit), blocks):
            cot_blocks[k] = block
        passed_on = [k for k in range(n_c) if k >> bit & 1 and k not in owned(bit)]
        if bit == 0:
            att_blocks.append(att_block)
            continue
        message = jnp.concatenate([cot_blocks[k] for k in passed_on] + att_blocks[1:], axis=0)
        if bit == bits[-1]:
            grad_act = dot(jnp.concatenate([cot_a, cot_b], axis=0), w_down, NT)
            normed_a = after(normed_a, grad_act, message)
        blocks = split(exchange(message, "ctx", 1 << bit))
        for k, block in zip(passed_on, blocks):
            cot_blocks[k] = block
        att_blocks.extend([att_block] + blocks[len(passed_on) :])
    normed_b = beside(normed_a)

    pay = gate_up_call(normed_a, normed_b, w_gate, w_up, grad_act)
    keep, give = normed_grad_call(pay, w_gate, w_up)
    total = pair_sum(keep, give)
    terms = scatter_rows(total)

    cot_cols = after(jnp.concatenate(cot_blocks, axis=0), total)
    cot_side = beside(cot_cols)

    late, normed_late = after((pay, normed_a), total)
    normed_blocks = column_blocks(c_ref, normed_late, n_c)

    class Half:
        def __init__(self, side):
            self.side = side
            self.order = list(bits) if side == 0 else list(bits)[::-1]
            lanes = slice(side * cols // 2, (side + 1) * cols // 2)
            self.columns = [block[:, lanes] for block in normed_blocks]
            self.arrays = [late]
            self.rows = {0: (0, side * pair, 0)}

        def row(self, k):
            array, start, at = self.rows[k]
            return self.arrays[array][start : start + pair, at : at + 3 * hidden_units]

        def message(self, step):
            bit = self.order[step]
            self.held = list(self.rows)
            self.moving = [k for k in range(n_c) if k >> bit & 1]
            parts = [self.row(k) for k in self.held] + [self.columns[k] for k in self.moving]
            return jnp.concatenate(parts, axis=1)

        def send(self, step, message):
            bit = self.order[step]
            self.arrays.append(exchange(message, "ctx", 1 << bit))
            at = 0
            for k in self.held:
                self.rows[k | 1 << bit] = (len(self.arrays) - 1, 0, at)
                at += 3 * hidden_units
            for k in self.moving:
                self.columns[k] = self.arrays[-1][:, at : at + cols // 2]
                at += cols // 2

    halves = [Half(0), Half(1)]
    for step in bits:
        messages = [h.message(step) for h in halves]
        if step == bits[-1]:
            down = dot(late[:, :hidden_units], w_down).astype(BF16)
            terms[0] = after(terms[0], messages[0], messages[1], down)
            grad_resid, grad_send, gain_part = norm_grad_call(cotangent, hidden, gain_row, terms)
        for h, message in zip(halves, messages):
            h.send(step, message)

    grad_a = gather_rows(grad_send)
    down_total = pair_sum(down[:pair], down[pair:])
    grad_a = after(grad_a, down_total, [h.arrays[-1] for h in halves])
    grad_b = beside(grad_a)
    down_late = after(down_total, grad_a)
    down_blocks = {m: down_late[m * share : (m + 1) * share] for m in range(half)}

    def crossing_down(blocks, bit):
        moving = [m for m in blocks if m >> bit & 1]
        message = jnp.concatenate([blocks[m] for m in moving], axis=0)
        return moving, exchange(message, "ffn", 2 << bit)

    def added_down(blocks, bit, moving, message):
        message = message.astype(F32)
        parts = {m ^ 1 << bit: message[i * share : (i + 1) * share] for i, m in enumerate(moving)}
        return {m: parts[m] + blocks[m].astype(F32) for m in parts}

    moving, message = crossing_down(down_blocks, 0)

    grad_queries, *parts = attention_grad_call(
        f_ref, q_rel, att, lse, gain_part, grad_a, grad_b, w_out, pieces, n_f
    )
    normed_cols = jnp.concatenate(
        [jnp.concatenate([h.columns[k] for h in halves], axis=1) for k in range(n_c)], axis=0
    )
    normed_side = beside(normed_cols)
    parts = [parts[0]] + [exchange(parts[k], "ctx", k) for k in range(1, n_c)]
    down_blocks = added_down(down_blocks, 0, moving, after(message, parts[0]))
    for bit in range(1, log2(half)):
        down_blocks = {m: block.astype(BF16) for m, block in down_blocks.items()}
        moving, message = crossing_down(down_blocks, bit)
        down_blocks = added_down(down_blocks, bit, moving, message)
    offset = len(halves[0].arrays)
    hidden_refs = halves[0].arrays + halves[1].arrays

    def hidden_part(i):
        pieces = []
        for side, h in enumerate(halves):
            for k in range(n_c):
                array, start, at = h.rows[k]
                pieces.append((array + side * offset, start, pair, at + i * hidden_units))
        return pieces

    columns = [(0, 0, n_c * pair, 0), (1, 0, n_c * pair, 0)]
    att_rows = [(k, 0, pair, 0) for k in range(n_c)] + [(k, 0, pair, width) for k in range(n_c)]
    normed_pair, shape = after((normed_cols, normed_side), parts[0]), (cols, hidden_units)
    grad_w_up = weight_grad_call(
        columns, normed_pair, hidden_part(2), hidden_refs, shape, 0, "grad_w_up"
    )
    grad_w_down = weight_grad_call(
        hidden_part(0), hidden_refs, columns, (cot_cols, cot_side), shape[::-1], 1, "grad_w_down"
    )
    own_chunks, beside_chunks = sum_call(f_ref, after(parts, grad_w_up), rows, n_f)
    grad_cols = to_columns(column_blocks(c_ref, after(grad_a, own_chunks), n_c))
    grad_cols = jnp.concatenate(grad_cols, axis=0)
    grad_side = beside(grad_cols)

    chunks = jnp.stack([own_chunks, beside(beside_chunks)], axis=1)
    chunks = [chunks[0]] + [exchange(chunks[m], "ffn", 2 * m) for m in range(1, half)]
    grad_w_gate = weight_grad_call(
        columns, after(normed_pair, own_chunks), hidden_part(1), hidden_refs, shape, 0, "grad_w_gate"
    )
    grad_keys, grad_values, grad_gain = heads_call(f_ref, after(chunks, grad_w_gate), depth, n_f)

    grad_w_out = weight_grad_call(
        att_rows, att_blocks, columns, (grad_cols, grad_side), (width, cols), 1, "grad_w_out"
    )

    mixed = (hidden.astype(F32) + down_blocks[0]).astype(BF16)

    return (
        mixed,
        grad_resid,
        grad_queries,
        grad_keys,
        grad_values,
        grad_gain.reshape(depth),
        grad_w_out,
        grad_w_gate,
        grad_w_up,
        grad_w_down,
    )


def solution(mesh):
    return jax.shard_map(
        body,
        mesh=mesh,
        in_specs=(
            P(("ctx", "ffn"), None),
            P("ctx", "ffn"),
            P("ctx", None),
            P("ctx", None),
            P("ffn", None),
            P(),
            P(None, "ffn"),
            P(None, "ffn"),
            P("ffn", None),
            P(("ctx", "ffn"), None),
            P("ctx"),
            P(),
        ),
        out_specs=(
            P(("ctx", "ffn"), None),
            P(("ctx", "ffn"), None),
            P("ctx", "ffn"),
            P(("ctx", "ffn"), None),
            P(("ctx", "ffn"), None),
            P(),
            P("ffn", "ctx"),
            P("ctx", "ffn"),
            P("ctx", "ffn"),
            P("ffn", "ctx"),
        ),
        check_vma=False,
    )
```

```python
import functools
import math

import jax
import jax.numpy as jnp
from jax import lax
from jax.experimental import pallas as pl
from jax.experimental.pallas import tpu as pltpu
from jax.sharding import PartitionSpec as P

QUERY_HEADS = 32
KEY_VALUE_HEADS = 8
HEAD_WIDTH = 128
STRIPE = 64

masked_fill = -1e30
norm_eps = 1e-05
score_scale = 1.0 / math.sqrt(HEAD_WIDTH)

F32 = jnp.float32
BF16 = jnp.bfloat16
NN = (((1,), (0,)), ((), ()))
NT = (((1,), (1,)), ((), ()))
TN = (((0,), (0,)), ((), ()))
VMEM = pl.BlockSpec(memory_space=pltpu.VMEM)
SMEM = pl.BlockSpec(memory_space=pltpu.SMEM)
ANY = pl.BlockSpec(memory_space=pl.ANY)


def dot(a, b, dims=NN):
    return lax.dot_general(a, b, dims, preferred_element_type=F32)


def params(megabytes=48):
    return pltpu.CompilerParams(vmem_limit_bytes=megabytes * 1024 * 1024)


def cost(microseconds):
    return pl.CostEstimate(
        flops=int(microseconds * 5e8), bytes_accessed=int(microseconds * 2e6), transcendentals=0
    )


def fetch(sources, targets, sems):
    copies = [pltpu.make_async_copy(s, t, sems.at[i]) for i, (s, t) in enumerate(zip(sources, targets))]
    for copy in copies:
        copy.start()
    return copies


def scratch_like(*arrays):
    return [pltpu.VMEM(a.shape, a.dtype) for a in arrays] + [
        pltpu.SemaphoreType.DMA((len(arrays),))
    ]


def log2(n):
    assert n & (n - 1) == 0
    return n.bit_length() - 1


def relative_rows(f, rows, n_f):
    share, half = rows // n_f, n_f // 2
    r = lax.broadcasted_iota(jnp.int32, (rows, rows), 0)
    natural = lax.broadcasted_iota(jnp.int32, (rows, rows), 1)
    j = lax.shift_right_logical(r, log2(share))
    k = lax.shift_left(j & (half - 1), 1) | lax.shift_right_logical(j, log2(half))
    return natural == lax.shift_left(k ^ f, log2(share)) + (r & (share - 1))


def visibility(same_row, pieces, rows):
    coded = [piece[2 * rows :, :].astype(F32) for piece in pieces]
    key_pos = jnp.concatenate([t[0:1] * STRIPE + t[1:2] for t in coded], axis=1)
    key_seg = jnp.concatenate([t[2:3] for t in coded], axis=1)

    def to_column(row):
        return jnp.sum(jnp.where(same_row, row[:, :rows], 0.0), axis=1, keepdims=True)

    return (key_pos <= to_column(key_pos)) & (key_seg == to_column(key_seg))


def keys_and_values(pieces, rows):
    return (
        jnp.concatenate([p[:rows] for p in pieces], axis=0),
        jnp.concatenate([p[rows : 2 * rows] for p in pieces], axis=0),
    )


def prepare_kernel(
    n_f, f_ref, group_ref, q_hbm, k_hbm, v_hbm, pos_hbm, doc_hbm, q_out, payload, *scratch
):
    q_ref, pos_ref, doc_ref, sems = scratch
    rows = q_ref.shape[0]
    cols = pl.ds(pl.multiple_of(group_ref[0] * HEAD_WIDTH, HEAD_WIDTH), HEAD_WIDTH)
    copies = fetch(
        [pos_hbm, doc_hbm, q_hbm, k_hbm.at[:, cols], v_hbm.at[:, cols]],
        [pos_ref, doc_ref, q_ref, payload.at[pl.ds(0, rows)], payload.at[pl.ds(rows, rows)]],
        sems,
    )
    same_row = relative_rows(f_ref[0], rows, n_f)
    line = lax.broadcasted_iota(jnp.int32, (16, rows), 0)
    copies[0].wait()
    copies[1].wait()
    pos = pos_ref[...]
    total = doc_ref.shape[1]
    where_is = lax.broadcasted_iota(jnp.int32, (total, rows), 0) == pos
    docs = jnp.broadcast_to(doc_ref[...].astype(F32), (8, total)).astype(BF16)
    seg = dot(docs, where_is.astype(F32).astype(BF16))[0:1]
    high = lax.shift_right_logical(pos, log2(STRIPE))
    low = pos & (STRIPE - 1)
    coded = jnp.where(line == 0, high.astype(F32), jnp.where(line == 1, low.astype(F32), 0.0))
    payload[2 * rows :, :] = jnp.where(line == 2, seg, coded).astype(BF16)
    copies[2].wait()
    q_out[...] = dot(same_row.astype(F32).astype(BF16), q_ref[...]).astype(BF16)
    copies[3].wait()
    copies[4].wait()


def prepare_call(f, group, queries, keys_in, values_in, pos_row, doc_row, n_f):
    rows = queries.shape[0]
    assert rows == HEAD_WIDTH
    return pl.pallas_call(
        functools.partial(prepare_kernel, n_f),
        out_shape=(
            jax.ShapeDtypeStruct(queries.shape, BF16),
            jax.ShapeDtypeStruct((2 * rows + 16, HEAD_WIDTH), BF16),
        ),
        in_specs=[SMEM, SMEM] + [ANY] * 5,
        out_specs=[VMEM] * 2,
        scratch_shapes=scratch_like(queries, pos_row, doc_row)[:-1]
        + [pltpu.SemaphoreType.DMA((5,))],
        compiler_params=params(58),
        cost_estimate=cost(2),
        name="prepare_attention",
    )(f, group, queries, keys_in, values_in, pos_row, doc_row)


def attention_kernel(n_f, n_c, f_ref, *refs):
    sources, refs = refs[: n_c + 2], refs[n_c + 2 :]
    (keep_ref, give_ref, att_ref, lse_ref), scratch, sems = refs[:4], refs[4:-1], refs[-1]
    copies = fetch(sources, scratch, sems)
    q_ref, pieces, w_ref = scratch[0], scratch[1:-1], scratch[-1]
    for copy in copies[:-1]:
        copy.wait()
    rows, width = q_ref.shape
    same_row = relative_rows(f_ref[0], rows, n_f)
    visible = visibility(same_row, pieces, rows)
    keys, values = keys_and_values(pieces, rows)
    q = q_ref[...]
    lane = lax.broadcasted_iota(jnp.int32, (rows, HEAD_WIDTH), 1)
    log_totals = jnp.zeros((rows, HEAD_WIDTH), F32)
    for h in range(width // HEAD_WIDTH):
        cols = slice(h * HEAD_WIDTH, (h + 1) * HEAD_WIDTH)
        scores = jnp.where(visible, dot(q[:, cols], keys, NT) * score_scale, masked_fill)
        row_max = jnp.max(scores, axis=1, keepdims=True)
        weights = jnp.exp(scores - row_max)
        row_total = jnp.sum(weights, axis=1, keepdims=True)
        att_ref[:, cols] = (dot(weights.astype(BF16), values) / row_total).astype(BF16)
        log_totals = jnp.where(lane == h, row_max + jnp.log(row_total), log_totals)
    lse_ref[...] = log_totals
    copies[-1].wait()
    att = att_ref[...]
    tile = 512
    for start in range(0, w_ref.shape[1], tile):
        out = dot(att, w_ref[:, start : start + tile]).astype(BF16)
        keep_ref[:, start : start + tile] = out[: rows // 2]
        give_ref[:, start : start + tile] = out[rows // 2 :]


def attention_call(f, queries, w_out, pieces, n_f):
    rows, width = queries.shape
    depth = w_out.shape[1]
    half = jax.ShapeDtypeStruct((rows // 2, depth), BF16)
    att = jax.ShapeDtypeStruct((rows, width), BF16)
    lse = jax.ShapeDtypeStruct((rows, HEAD_WIDTH), F32)
    return pl.pallas_call(
        functools.partial(attention_kernel, n_f, len(pieces)),
        out_shape=(half, half, att, lse),
        in_specs=[SMEM] + [ANY] * (2 + len(pieces)),
        out_specs=[VMEM] * 4,
        scratch_shapes=scratch_like(queries, *pieces, w_out),
        compiler_params=params(56),
        cost_estimate=cost(4),
        name="attention_and_projection",
    )(f, queries, *pieces, w_out)


def fold(row):
    width = 2 * HEAD_WIDTH
    return [row[:, i : i + width] for i in range(0, row.shape[1], width)]


def attention_grad_kernel(n_f, n_c, f_ref, *refs):
    pieces, refs = refs[:n_c], refs[n_c:]
    q_ref, att_ref, lse_ref, gain_ref, ga_ref, gb_ref, w_ref = refs[:7]
    dq_ref, dkv_refs = refs[7], refs[8:]
    rows, width = q_ref.shape
    same_row = relative_rows(f_ref[0], rows, n_f)
    visible = visibility(same_row, pieces, rows)
    keys, values = keys_and_values(pieces, rows)
    order = same_row.astype(F32).astype(BF16)
    q = q_ref[...]
    grad_rows = jnp.concatenate([ga_ref[...], gb_ref[...]], axis=0)
    grad_att = dot(grad_rows, w_ref[...], NT).astype(BF16)
    grad_keys = jnp.zeros(keys.shape, F32)
    grad_values = jnp.zeros(keys.shape, F32)
    grad_q = []
    for h in range(width // HEAD_WIDTH):
        cols = slice(h * HEAD_WIDTH, (h + 1) * HEAD_WIDTH)
        g = grad_att[:, cols]
        scores = jnp.where(visible, dot(q[:, cols], keys, NT) * score_scale, masked_fill)
        probs = jnp.exp(scores - lse_ref[:, h : h + 1])
        delta = jnp.sum(g.astype(F32) * att_ref[:, cols].astype(F32), axis=1, keepdims=True)
        grad_scores = (probs * (dot(g, values, NT) - delta)).astype(BF16)
        grad_q.append((dot(grad_scores, keys) * score_scale).astype(BF16))
        grad_keys = grad_keys + dot(grad_scores, q[:, cols], TN)
        grad_values = grad_values + dot(probs.astype(BF16), g, TN)
    dq_ref[...] = dot(order, jnp.concatenate(grad_q, axis=1), TN).astype(BF16)
    high = gain_ref[...].astype(BF16)
    low = (gain_ref[...] - high.astype(F32)).astype(BF16)
    lines = fold(high) + fold(low)
    for k, dkv_ref in enumerate(dkv_refs):
        part = slice(k * rows, (k + 1) * rows)
        dkv_ref[:rows, :HEAD_WIDTH] = (grad_keys[part] * score_scale).astype(BF16)
        dkv_ref[:rows, HEAD_WIDTH:] = grad_values[part].astype(BF16)
        for i, line in enumerate(lines):
            dkv_ref[rows + i : rows + i + 1, :] = line


def attention_grad_call(f, queries, att, lse, gain, grad_a, grad_b, w_out, pieces, n_f):
    rows, width = queries.shape
    n_c = len(pieces)
    dkv = jax.ShapeDtypeStruct((rows + gain.shape[1] // HEAD_WIDTH, 2 * HEAD_WIDTH), BF16)
    return pl.pallas_call(
        functools.partial(attention_grad_kernel, n_f, n_c),
        out_shape=(jax.ShapeDtypeStruct((rows, width), BF16),) + (dkv,) * n_c,
        in_specs=[SMEM] + [VMEM] * (7 + n_c),
        out_specs=(VMEM,) * (1 + n_c),
        compiler_params=params(24),
        cost_estimate=cost(4),
        name="attention_gradients",
    )(f, *pieces, queries, att, lse, gain, grad_a, grad_b, w_out)


def pair_sum_kernel(keep_ref, recv_ref, out_ref):
    out_ref[...] = (keep_ref[...].astype(F32) + recv_ref[...].astype(F32)).astype(BF16)


def pair_sum_call(keep, received):
    return pl.pallas_call(
        pair_sum_kernel,
        out_shape=jax.ShapeDtypeStruct(keep.shape, BF16),
        in_specs=[VMEM] * 2,
        out_specs=VMEM,
        compiler_params=params(8),
        cost_estimate=cost(1),
        name="pair_sum",
    )(keep, received)


def norm_kernel(resid_ref, gain_ref, *refs):
    terms, (hidden_ref, normed_ref) = refs[:-2], refs[-2:]
    total = resid_ref[...].astype(F32)
    total = total + functools.reduce(jnp.add, [t[...].astype(F32) for t in terms])
    hidden = total.astype(BF16)
    hidden_ref[...] = hidden
    hidden = hidden.astype(F32)
    inv_rms = lax.rsqrt(jnp.mean(hidden * hidden, axis=1, keepdims=True) + norm_eps)
    normed_ref[...] = (hidden * inv_rms * gain_ref[...]).astype(BF16)


def norm_call(resid, gain_row, terms):
    out = jax.ShapeDtypeStruct(resid.shape, BF16)
    return pl.pallas_call(
        norm_kernel,
        out_shape=(out, out),
        in_specs=[VMEM] * (2 + len(terms)),
        out_specs=[VMEM] * 2,
        compiler_params=params(8),
        cost_estimate=cost(8),
        name="residual_and_norm",
    )(resid, gain_row, *terms)


def norm_grad_kernel(cot_ref, hidden_ref, gain_ref, *refs):
    terms, (grad_ref, copy_ref, gain_grad_ref) = refs[:-3], refs[-3:]
    grad_normed = functools.reduce(jnp.add, [t[...].astype(F32) for t in terms])
    hidden = hidden_ref[...].astype(F32)
    inv_rms = lax.rsqrt(jnp.mean(hidden * hidden, axis=1, keepdims=True) + norm_eps)
    gained = grad_normed * gain_ref[...]
    inv_cube = inv_rms * inv_rms * inv_rms
    grad = (
        cot_ref[...].astype(F32)
        + inv_rms * gained
        - hidden * inv_cube * jnp.mean(gained * hidden, axis=1, keepdims=True)
    ).astype(BF16)
    grad_ref[...] = grad
    copy_ref[...] = grad
    gain_grad_ref[...] = jnp.sum(grad_normed * hidden * inv_rms, axis=0, keepdims=True)


def norm_grad_call(cot, hidden, gain_row, terms):
    return pl.pallas_call(
        norm_grad_kernel,
        out_shape=(
            jax.ShapeDtypeStruct(cot.shape, BF16),
            jax.ShapeDtypeStruct(cot.shape, BF16),
            jax.ShapeDtypeStruct(gain_row.shape, F32),
        ),
        in_specs=[VMEM] * (3 + len(terms)),
        out_specs=[VMEM] * 3,
        compiler_params=params(8),
        cost_estimate=cost(8),
        name="norm_gradients",
    )(cot, hidden, gain_row, *terms)


def gate_up_kernel(xa_ref, xb_ref, wg_ref, wu_ref, ga_ref, out_ref):
    width = wg_ref.shape[1]
    x = jnp.concatenate([xa_ref[...], xb_ref[...]], axis=0)
    tile = 256
    for start in range(0, width, tile):
        end = min(start + tile, width)
        gate, up = dot(x, wg_ref[:, start:end]), dot(x, wu_ref[:, start:end])
        grad_act = ga_ref[:, start:end]
        sig = jax.nn.sigmoid(gate)
        out_ref[:, start:end] = (gate * sig * up).astype(BF16)
        grad_gate = grad_act * up * sig * (1.0 + gate * (1.0 - sig))
        out_ref[:, width + start : width + end] = grad_gate.astype(BF16)
        out_ref[:, 2 * width + start : 2 * width + end] = (grad_act * gate * sig).astype(BF16)


def gate_up_call(xa, xb, w_gate, w_up, grad_act):
    depth, width = w_gate.shape
    rows = grad_act.shape[0]
    return pl.pallas_call(
        gate_up_kernel,
        out_shape=jax.ShapeDtypeStruct((rows, 3 * width), BF16),
        in_specs=[VMEM] * 5,
        out_specs=VMEM,
        compiler_params=params(24),
        cost_estimate=cost(2),
        name="gate_up_and_gradients",
    )(xa, xb, w_gate, w_up, grad_act)


def normed_grad_kernel(pay_ref, wg_ref, wu_ref, keep_ref, give_ref):
    depth, width = wg_ref.shape
    half = keep_ref.shape[0]
    grad_gate, grad_up = pay_ref[:, width : 2 * width], pay_ref[:, 2 * width :]
    tile = 1024
    for start in range(0, depth, tile):
        at = slice(start, start + tile)
        out = dot(wg_ref[at, :], grad_gate, NT) + dot(wu_ref[at, :], grad_up, NT)
        out = out.T.astype(BF16)
        keep_ref[:, at] = out[:half]
        give_ref[:, at] = out[half:]


def normed_grad_call(pay, w_gate, w_up):
    depth, width = w_gate.shape
    rows = pay.shape[0]
    out = jax.ShapeDtypeStruct((rows // 2, depth), BF16)
    return pl.pallas_call(
        normed_grad_kernel,
        out_shape=(out, out),
        in_specs=[VMEM] * 3,
        out_specs=[VMEM] * 2,
        compiler_params=params(24),
        cost_estimate=cost(2),
        name="normed_gradients",
    )(pay, w_gate, w_up)


def column_blocks_kernel(c_ref, a_ref, *out_refs):
    cols = a_ref.shape[1] // len(out_refs)
    for k, out_ref in enumerate(out_refs):
        start = pl.multiple_of((c_ref[0] ^ k) * cols, 128)
        out_ref[...] = a_ref[:, pl.ds(start, cols)]


def column_blocks(c, a, n_c):
    rows, depth = a.shape
    return pl.pallas_call(
        column_blocks_kernel,
        out_shape=(jax.ShapeDtypeStruct((rows, depth // n_c), BF16),) * n_c,
        in_specs=[SMEM, VMEM],
        out_specs=(VMEM,) * n_c,
        compiler_params=params(8),
        cost_estimate=cost(1),
        name="column_blocks",
    )(c, a)


def take(refs, pieces, width):
    return jnp.concatenate([refs[i][r : r + n, at : at + width] for i, r, n, at in pieces], axis=0)


def weight_grad_kernel(left, right, n_left, tiled, *refs):
    operands, (out_hbm, out_ref, sems) = refs[:-3], refs[-3:]
    height, width = out_ref.shape
    left_refs, right_refs = operands[:n_left], operands[n_left:]
    tile = 256
    copies = []
    fixed = take(right_refs, right, width) if tiled == 0 else take(left_refs, left, height)
    for n, at in enumerate(range(0, out_ref.shape[tiled], tile)):
        size = min(tile, out_ref.shape[tiled] - at)
        if tiled == 0:
            moving = take(left_refs, [(i, r, m, first + at) for i, r, m, first in left], size)
            where = (pl.ds(at, size), slice(None))
            out_ref[where] = dot(moving, fixed, TN)
        else:
            moving = take(right_refs, [(i, r, m, first + at) for i, r, m, first in right], size)
            where = (slice(None), pl.ds(at, size))
            out_ref[where] = dot(fixed, moving, TN)
        copies.append(pltpu.make_async_copy(out_ref.at[where], out_hbm.at[where], sems.at[n]))
        copies[-1].start()
    for copy in copies:
        copy.wait()


def weight_grad_call(left, left_refs, right, right_refs, widths, tiled, name):
    return pl.pallas_call(
        functools.partial(weight_grad_kernel, left, right, len(left_refs), tiled),
        out_shape=jax.ShapeDtypeStruct(widths, F32),
        in_specs=[VMEM] * (len(left_refs) + len(right_refs)),
        out_specs=ANY,
        scratch_shapes=[
            pltpu.VMEM(widths, F32),
            pltpu.SemaphoreType.DMA((-(-widths[tiled] // 256),)),
        ],
        compiler_params=params(20),
        cost_estimate=cost(3),
        name=name,
    )(*left_refs, *right_refs)


def tree_sum(values):
    while len(values) > 1:
        values = [values[i] + values[i + 1] for i in range(0, len(values), 2)]
    return values[0]


def sum_kernel(n_f, rows, f_ref, *refs):
    parts, (own_ref, beside_ref, total_ref) = refs[:-3], refs[-3:]
    share, lines = rows // n_f, (parts[0].shape[0] - rows) // 2
    total_ref[...] = tree_sum([p[:rows, :].astype(F32) for p in parts])
    gain = tree_sum(
        [p[rows : rows + lines, :].astype(F32) + p[rows + lines :, :].astype(F32) for p in parts]
    )
    high = gain.astype(BF16)
    low = (gain - high.astype(F32)).astype(BF16)
    for k in range(n_f):
        out_ref = (own_ref, beside_ref)[k % 2]
        start = pl.multiple_of((f_ref[0] ^ k) * share, share)
        out_ref[k // 2, :lines, :] = high
        out_ref[k // 2, lines : 2 * lines, :] = low
        out_ref[k // 2, 2 * lines :, :] = total_ref[pl.ds(start, share), :].astype(BF16)


def sum_call(f, parts, rows, n_f):
    lines = parts[0].shape[0] - rows
    out = jax.ShapeDtypeStruct((n_f // 2, lines + rows // n_f, 2 * HEAD_WIDTH), BF16)
    return pl.pallas_call(
        functools.partial(sum_kernel, n_f, rows),
        out_shape=(out, out),
        in_specs=[SMEM] + [VMEM] * len(parts),
        out_specs=(VMEM, VMEM),
        scratch_shapes=[pltpu.VMEM((rows, 2 * HEAD_WIDTH), F32)],
        compiler_params=params(8),
        cost_estimate=cost(1),
        name="sum_over_ctx",
    )(f, *parts)


def heads_kernel(n_f, f_ref, *refs):
    in_refs, (dk_ref, dv_ref, gain_ref) = refs[:-3], refs[-3:]
    per_head = n_f // KEY_VALUE_HEADS
    width = 2 * HEAD_WIDTH
    lines = gain_ref.shape[1] // width
    chunks = [(ref, i) for ref in in_refs for i in range(2)]
    for k in range(0, n_f, per_head):
        total = tree_sum([r[i, 2 * lines :, :].astype(F32) for r, i in chunks[k : k + per_head]])
        head = lax.shift_right_logical(f_ref[0] ^ k, log2(per_head))
        at = pl.ds(pl.multiple_of(head * HEAD_WIDTH, HEAD_WIDTH), HEAD_WIDTH)
        dk_ref[:, at] = total[:, :HEAD_WIDTH]
        dv_ref[:, at] = total[:, HEAD_WIDTH:]
    gain = tree_sum(
        [
            r[i, :lines, :].astype(F32) + r[i, lines : 2 * lines, :].astype(F32)
            for r, i in chunks
        ]
    )
    for i in range(lines):
        gain_ref[:, i * width : (i + 1) * width] = gain[i : i + 1]


def heads_call(f, pairs, depth, n_f):
    share = pairs[0].shape[1] - depth // HEAD_WIDTH
    out = jax.ShapeDtypeStruct((share, KEY_VALUE_HEADS * HEAD_WIDTH), F32)
    return pl.pallas_call(
        functools.partial(heads_kernel, n_f),
        out_shape=(out, out, jax.ShapeDtypeStruct((1, depth), F32)),
        in_specs=[SMEM] + [VMEM] * len(pairs),
        out_specs=[VMEM] * 3,
        compiler_params=params(8),
        cost_estimate=cost(1),
        name="place_heads",
    )(f, *pairs)


def body(
    resid_in,
    queries,
    keys_in,
    value_rows_input,
    w_out,
    norm_gain,
    w_gate,
    w_up,
    w_down,
    cotangent,
    positions,
    doc_ids,
):
    rows = queries.shape[0]
    heads = queries.shape[1] // HEAD_WIDTH
    n_c, n_f = lax.axis_size("ctx"), lax.axis_size("ffn")
    c, f = lax.axis_index("ctx"), lax.axis_index("ffn")
    share, half = rows // n_f, n_f // 2
    depth = resid_in.shape[1]
    hidden_units = w_gate.shape[1]
    group = f * heads // (QUERY_HEADS // KEY_VALUE_HEADS)
    gain_row = norm_gain.reshape(1, depth)

    def exchange(x, axis, k):
        return lax.ppermute(x, axis, [(i, i ^ k) for i in range(lax.axis_size(axis))])

    def gather_rows(x):
        return jnp.concatenate([x] + [exchange(x, "ffn", 2 * m) for m in range(1, half)], axis=0)

    def beside(x):
        return exchange(x, "ffn", 1)

    def pair_sum(keep, give):
        return (keep.astype(F32) + beside(give).astype(F32)).astype(BF16)

    def scatter_rows(total):
        blocks = [total[m * share : (m + 1) * share] for m in range(half)]
        return [blocks[0]] + [exchange(blocks[m], "ffn", 2 * m) for m in range(1, half)]

    def after(x, *earlier):
        return lax.optimization_barrier((x, earlier))[0]

    bits = range(log2(n_c))

    def to_columns(blocks):
        return [blocks[0]] + [exchange(blocks[k], "ctx", k) for k in range(1, n_c)]

    cols = depth // n_c
    width = heads * HEAD_WIDTH
    pair = rows // 2
    f_ref = f.astype(jnp.int32).reshape(1)
    c_ref = c.astype(jnp.int32).reshape(1)
    q_rel, payload = prepare_call(
        f_ref,
        group.astype(jnp.int32).reshape(1),
        queries,
        keys_in,
        value_rows_input,
        positions.reshape(1, -1),
        doc_ids.reshape(1, -1),
        n_f,
    )
    pieces = [payload] + [exchange(payload, "ctx", k) for k in range(1, n_c)]
    cot_a = gather_rows(cotangent)

    keep, give, att, lse = attention_call(f_ref, q_rel, w_out, pieces, n_f)
    total = after(pair_sum_call(keep, beside(give)), cot_a)
    terms = scatter_rows(total)
    cot_b = beside(after(cot_a, total))
    terms[0] = after(terms[0], cot_b)

    assert 2 * width == cols
    cot_late = after(cot_a, cot_b)
    cot_blocks = list(column_blocks(c_ref, cot_late, n_c))
    att_blocks = [jnp.concatenate([att[:pair], att[pair:]], axis=1)]

    def split(message):
        return [message[i : i + pair] for i in range(0, message.shape[0], pair)]

    def owned(bit):
        return [k for k in range(n_c) if k >> bit & 1 and not k & ((1 << bit) - 1)]

    first_messages = [
        exchange(
            jnp.concatenate([cot_blocks[k] for k in owned(bit)] + att_blocks, axis=0),
            "ctx",
            1 << bit,
        )
        for bit in bits
    ]
    terms[0] = after(terms[0], first_messages)
    hidden, normed = norm_call(resid_in, gain_row, terms)
    normed_a = gather_rows(normed)
    for bit in bits:
        *blocks, att_block = split(first_messages[bit])
        for k, block in zip(owned(bit), blocks):
            cot_blocks[k] = block
        passed_on = [k for k in range(n_c) if k >> bit & 1 and k not in owned(bit)]
        if bit == 0:
            att_blocks.append(att_block)
            continue
        message = jnp.concatenate([cot_blocks[k] for k in passed_on] + att_blocks[1:], axis=0)
        if bit == bits[-1]:
            grad_act = dot(jnp.concatenate([cot_a, cot_b], axis=0), w_down, NT)
            normed_a = after(normed_a, grad_act, message)
        blocks = split(exchange(message, "ctx", 1 << bit))
        for k, block in zip(passed_on, blocks):
            cot_blocks[k] = block
        att_blocks.extend([att_block] + blocks[len(passed_on) :])
    normed_b = beside(normed_a)

    pay = gate_up_call(normed_a, normed_b, w_gate, w_up, grad_act)
    keep, give = normed_grad_call(pay, w_gate, w_up)
    total = pair_sum(keep, give)
    terms = scatter_rows(total)

    cot_cols = after(jnp.concatenate(cot_blocks, axis=0), total)
    cot_side = beside(cot_cols)

    late, normed_late = after((pay, normed_a), total)
    normed_blocks = column_blocks(c_ref, normed_late, n_c)

    class Half:
        def __init__(self, side):
            self.side = side
            self.order = list(bits) if side == 0 else list(bits)[::-1]
            lanes = slice(side * cols // 2, (side + 1) * cols // 2)
            self.columns = [block[:, lanes] for block in normed_blocks]
            self.arrays = [late]
            self.rows = {0: (0, side * pair, 0)}

        def row(self, k):
            array, start, at = self.rows[k]
            return self.arrays[array][start : start + pair, at : at + 3 * hidden_units]

        def message(self, step):
            bit = self.order[step]
            self.held = list(self.rows)
            self.moving = [k for k in range(n_c) if k >> bit & 1]
            parts = [self.row(k) for k in self.held] + [self.columns[k] for k in self.moving]
            return jnp.concatenate(parts, axis=1)

        def send(self, step, message):
            bit = self.order[step]
            self.arrays.append(exchange(message, "ctx", 1 << bit))
            at = 0
            for k in self.held:
                self.rows[k | 1 << bit] = (len(self.arrays) - 1, 0, at)
                at += 3 * hidden_units
            for k in self.moving:
                self.columns[k] = self.arrays[-1][:, at : at + cols // 2]
                at += cols // 2

    halves = [Half(0), Half(1)]
    for step in bits:
        messages = [h.message(step) for h in halves]
        if step == bits[-1]:
            down = dot(late[:, :hidden_units], w_down).astype(BF16)
            terms[0] = after(terms[0], messages[0], messages[1], down)
            grad_resid, grad_send, gain_part = norm_grad_call(cotangent, hidden, gain_row, terms)
        for h, message in zip(halves, messages):
            h.send(step, message)

    grad_a = gather_rows(grad_send)
    down_total = pair_sum(down[:pair], down[pair:])
    grad_a = after(grad_a, down_total, [h.arrays[-1] for h in halves])
    grad_b = beside(grad_a)
    down_late = after(down_total, grad_a)
    down_blocks = {m: down_late[m * share : (m + 1) * share] for m in range(half)}

    def crossing_down(blocks, bit):
        moving = [m for m in blocks if m >> bit & 1]
        message = jnp.concatenate([blocks[m] for m in moving], axis=0)
        return moving, exchange(message, "ffn", 2 << bit)

    def added_down(blocks, bit, moving, message):
        message = message.astype(F32)
        parts = {m ^ 1 << bit: message[i * share : (i + 1) * share] for i, m in enumerate(moving)}
        return {m: parts[m] + blocks[m].astype(F32) for m in parts}

    moving, message = crossing_down(down_blocks, 0)

    grad_queries, *parts = attention_grad_call(
        f_ref, q_rel, att, lse, gain_part, grad_a, grad_b, w_out, pieces, n_f
    )
    normed_cols = jnp.concatenate(
        [jnp.concatenate([h.columns[k] for h in halves], axis=1) for k in range(n_c)], axis=0
    )
    normed_side = beside(normed_cols)
    parts = [parts[0]] + [exchange(parts[k], "ctx", k) for k in range(1, n_c)]
    down_blocks = added_down(down_blocks, 0, moving, after(message, parts[0]))
    for bit in range(1, log2(half)):
        down_blocks = {m: block.astype(BF16) for m, block in down_blocks.items()}
        moving, message = crossing_down(down_blocks, bit)
        down_blocks = added_down(down_blocks, bit, moving, message)
    offset = len(halves[0].arrays)
    hidden_refs = halves[0].arrays + halves[1].arrays

    def hidden_part(i):
        pieces = []
        for side, h in enumerate(halves):
            for k in range(n_c):
                array, start, at = h.rows[k]
                pieces.append((array + side * offset, start, pair, at + i * hidden_units))
        return pieces

    columns = [(0, 0, n_c * pair, 0), (1, 0, n_c * pair, 0)]
    att_rows = [(k, 0, pair, 0) for k in range(n_c)] + [(k, 0, pair, width) for k in range(n_c)]
    normed_pair, shape = after((normed_cols, normed_side), parts[0]), (cols, hidden_units)
    grad_w_up = weight_grad_call(
        columns, normed_pair, hidden_part(2), hidden_refs, shape, 0, "grad_w_up"
    )
    grad_w_down = weight_grad_call(
        hidden_part(0), hidden_refs, columns, (cot_cols, cot_side), shape[::-1], 1, "grad_w_down"
    )
    own_chunks, beside_chunks = sum_call(f_ref, after(parts, grad_w_up), rows, n_f)
    grad_cols = to_columns(column_blocks(c_ref, after(grad_a, own_chunks), n_c))
    grad_cols = jnp.concatenate(grad_cols, axis=0)
    grad_side = beside(grad_cols)

    chunks = jnp.stack([own_chunks, beside(beside_chunks)], axis=1)
    chunks = [chunks[0]] + [exchange(chunks[m], "ffn", 2 * m) for m in range(1, half)]
    grad_w_gate = weight_grad_call(
        columns, after(normed_pair, own_chunks), hidden_part(1), hidden_refs, shape, 0, "grad_w_gate"
    )
    grad_keys, grad_values, grad_gain = heads_call(f_ref, after(chunks, grad_w_gate), depth, n_f)

    grad_w_out = weight_grad_call(
        att_rows, att_blocks, columns, (grad_cols, grad_side), (width, cols), 1, "grad_w_out"
    )

    mixed = (hidden.astype(F32) + down_blocks[0]).astype(BF16)

    return (
        mixed,
        grad_resid,
        grad_queries,
        grad_keys,
        grad_values,
        grad_gain.reshape(depth),
        grad_w_out,
        grad_w_gate,
        grad_w_up,
        grad_w_down,
    )


def solution(mesh):
    return jax.shard_map(
        body,
        mesh=mesh,
        in_specs=(
            P(("ctx", "ffn"), None),
            P("ctx", "ffn"),
            P("ctx", None),
            P("ctx", None),
            P("ffn", None),
            P(),
            P(None, "ffn"),
            P(None, "ffn"),
            P("ffn", None),
            P(("ctx", "ffn"), None),
            P("ctx"),
            P(),
        ),
        out_specs=(
            P(("ctx", "ffn"), None),
            P(("ctx", "ffn"), None),
            P("ctx", "ffn"),
            P(("ctx", "ffn"), None),
            P(("ctx", "ffn"), None),
            P(),
            P("ffn", "ctx"),
            P("ctx", "ffn"),
            P("ctx", "ffn"),
            P("ffn", "ctx"),
        ),
        check_vma=False,
    )
```
